1024 devices in a mesh: gx: 8 (over z_hi, core), gy: 16 (over y, x), gz: 8 (over z_lo).
Axes of the slice: x: 4, y: 4, z: 32 (z_hi: 4, z_lo: 8; z = z_hi * 8 + z_lo), core: 2. Of those that a mesh axis runs over, the one named last changes fastest.
Arguments:
- load: float32 [3, 64, 128, 1024], P(None, 'gz', 'gy', 'gx'), may hold values from -30 to 30
- classes: int32 [56, 112, 1016], P('gz', 'gy', 'gx'), may hold values from 0 to 63
- densities: float32 [64], replicated, may hold values from 0.2 to 1
Outputs:
- displacement: float32 [3, 64, 128, 1024], P(None, 'gz', 'gy', 'gx')
- residual: float32 [3, 64, 128, 1024], P(None, 'gz', 'gy', 'gx')
- search_direction: float32 [3, 64, 128, 1024], P(None, 'gz', 'gy', 'gx')
The draws below stay inside these ranges and needn't reach their ends.
All inputs are finite; a program needn't handle non-finite values.
Results may differ from the reference program's by a relative error of at most 0.0003.
Values sent between devices are 32-bit elements; how exact they have to be, the bound alone decides.
A program may use at most 32 MiB of HBM per device.

```python
import math
import jax
import jax.numpy as jnp
import numpy as np
from jax import lax

CX = 127
CY = 7
CZ = 7
NCLASS = 64
NX = 1016
NY = 112
NZ = 56
NODE_X = 1024
NODE_Y = 128
NODE_Z = 64
N_GX = 8
N_GY = 16
N_GZ = 8


def draw_load(key, part):
    key = jax.random.fold_in(key, 7)
    first = jax.random.fold_in(key, 0)
    position = jnp.arange(NODE_X, dtype=jnp.float32) / NODE_X
    ramp = jnp.exp(jnp.log(3.0) * position)
    extent = (3, NODE_Z, NODE_Y, NODE_X)
    values = jnp.clip(jax.random.normal(first, extent, jnp.float32), -6.0, 6.0)
    return (values * ramp).astype(jnp.float32)


def with_ends(values, key, smallest, largest):
    index_at = [jax.random.randint(jax.random.fold_in(key, axis), (), 0, length) for axis, length in enumerate(values.shape)]
    widest = values.shape.index(max(values.shape))
    next_to = index_at[:widest] + [(index_at[widest] + 1) % values.shape[widest]] + index_at[widest + 1:]
    return values.at[tuple(index_at)].set(smallest).at[tuple(next_to)].set(largest)


def setup_inputs(seed: int = 0) -> dict:
    key_of = jax.random.split(jax.random.key(seed), 4)
    load = draw_load(jax.random.fold_in(key_of[3], 71), 0)
    classes = with_ends(jax.random.randint(key_of[1], (NZ, NY, NX), 0, NCLASS), jax.random.fold_in(key_of[1], 1), 0, NCLASS - 1).astype(jnp.int32)
    densities = jnp.clip(jax.random.uniform(key_of[2], (NCLASS,), jnp.float32, 0.2, 1.0), 0.2, 1.0)
    return {"load": load, "classes": classes, "densities": densities}


soft_floor = 0.001

def element_stiffness():
    poisson = 0.3
    lame_first = poisson / ((1.0 + poisson) * (1.0 - 2.0 * poisson))
    shear = 0.5 / (1.0 + poisson)
    elastic = np.zeros((6, 6))
    elastic[:3, :3] = lame_first
    for axis_index in range(3):
        elastic[axis_index, axis_index] += 2.0 * shear
        elastic[3 + axis_index, 3 + axis_index] = shear
    gauss_points = [0.5 - 0.5 / math.sqrt(3.0), 0.5 + 0.5 / math.sqrt(3.0)]
    matrix = np.zeros((24, 24))
    for point_z in gauss_points:
        for point_y in gauss_points:
            for point_x in gauss_points:
                strain = np.zeros((6, 24))
                for corner in range(8):
                    bit_x = corner % 2
                    bit_y = corner // 2 % 2
                    bit_z = corner // 4
                    shape_x = 1 - bit_x + (2 * bit_x - 1) * point_x
                    shape_y = 1 - bit_y + (2 * bit_y - 1) * point_y
                    shape_z = 1 - bit_z + (2 * bit_z - 1) * point_z
                    grad_x = (2 * bit_x - 1) * shape_y * shape_z
                    grad_y = shape_x * (2 * bit_y - 1) * shape_z
                    grad_z = shape_x * shape_y * (2 * bit_z - 1)
                    column = 3 * corner
                    strain[0, column] = grad_x
                    strain[1, column + 1] = grad_y
                    strain[2, column + 2] = grad_z
                    strain[3, column] = grad_y
                    strain[3, column + 1] = grad_x
                    strain[4, column + 1] = grad_z
                    strain[4, column + 2] = grad_y
                    strain[5, column] = grad_z
                    strain[5, column + 2] = grad_x
                matrix += strain.T @ elastic @ strain / 8.0
    return matrix

def corner_offsets():
    return [(corner // 4, corner // 2 % 2, corner % 2) for corner in range(8)]

def apply_stiffness(field, stiffness, matrix):

    def layer(level):
        slab = lax.dynamic_slice_in_dim(field, level, 2, axis=1)
        weight = lax.dynamic_index_in_dim(stiffness, level, 0, keepdims=False)
        pieces = [slab[:, bit_z, bit_y:bit_y + NY, bit_x:bit_x + NX] for bit_z, bit_y, bit_x in corner_offsets()]
        gathered = jnp.stack(pieces, 0).reshape(24, NY * NX)
        result = jnp.dot(matrix, gathered, precision=lax.Precision.HIGHEST) * weight.reshape(1, NY * NX)
        result = result.reshape(8, 3, NY, NX)
        lower = jnp.zeros((3, NY + 1, NX + 1), field.dtype)
        upper = jnp.zeros((3, NY + 1, NX + 1), field.dtype)
        for corner, (bit_z, bit_y, bit_x) in enumerate(corner_offsets()):
            placed = jnp.pad(result[corner], ((0, 0), (bit_y, 1 - bit_y), (bit_x, 1 - bit_x)))
            if bit_z == 0:
                lower = lower + placed
            else:
                upper = upper + placed
        return jnp.stack([lower, upper], 1)
    parts = lax.map(layer, jnp.arange(NZ, dtype=jnp.int32))
    lower = jnp.moveaxis(parts[:, :, 0], 0, 1)
    upper = jnp.moveaxis(parts[:, :, 1], 0, 1)
    return jnp.pad(lower, ((0, 0), (0, 1), (0, 0), (0, 0))) + jnp.pad(upper, ((0, 0), (1, 0), (0, 0), (0, 0)))

def reference(load, classes, densities):
    matrix = jnp.asarray(element_stiffness(), jnp.float32)
    corner_diag = jnp.diagonal(matrix).reshape(8, 3)
    index_z = (jnp.arange(N_GZ, dtype=jnp.int32)[:, None] * CZ + jnp.arange(CZ + 1, dtype=jnp.int32)[None, :]).reshape(-1)
    index_y = (jnp.arange(N_GY, dtype=jnp.int32)[:, None] * CY + jnp.arange(CY + 1, dtype=jnp.int32)[None, :]).reshape(-1)
    index_x = (jnp.arange(N_GX, dtype=jnp.int32)[:, None] * CX + jnp.arange(CX + 1, dtype=jnp.int32)[None, :]).reshape(-1)
    where_z = index_z[:, None, None]
    where_y = index_y[None, :, None]
    where_x = index_x[None, None, :]
    force = jnp.zeros((3, NZ + 1, NY + 1, NX + 1), jnp.float32).at[:, where_z, where_y, where_x].add(load)
    rho = densities[classes]
    stiffness = soft_floor + rho * rho * rho * (1.0 - soft_floor)
    diagonal = jnp.zeros((3, NZ + 1, NY + 1, NX + 1), jnp.float32)
    for corner, (bit_z, bit_y, bit_x) in enumerate(corner_offsets()):
        term = corner_diag[corner][:, None, None, None] * stiffness[None]
        diagonal = diagonal + jnp.pad(term, ((0, 0), (bit_z, 1 - bit_z), (bit_y, 1 - bit_y), (bit_x, 1 - bit_x)))
    keep = (jnp.arange(NX + 1) > 0).astype(jnp.float32)[None, None, None, :]
    diagonal = jnp.where(keep > 0.5, diagonal, 1.0)
    start = keep * force
    preconditioned = start / diagonal
    rz_start = jnp.sum(start * preconditioned)
    image = keep * apply_stiffness(preconditioned, stiffness, matrix)
    curvature = jnp.sum(preconditioned * image)
    alpha = rz_start / curvature
    solution = alpha * preconditioned
    remaining = start - alpha * image
    scaled = remaining / diagonal
    rz_next = jnp.sum(remaining * scaled)
    direction = scaled + rz_next / rz_start * preconditioned
    return (solution[:, where_z, where_y, where_x], remaining[:, where_z, where_y, where_x], direction[:, where_z, where_y, where_x])
```

```python
import functools
import math

import jax
import jax.numpy as jnp
import numpy as np
from jax import lax
from jax.experimental import pallas as pl
from jax.experimental.pallas import tpu as pltpu
from jax.sharding import PartitionSpec as P

MESH = pl.DeviceIdType.MESH
soft_floor = 0.001
poisson = 0.3
lame = poisson / ((1.0 + poisson) * (1.0 - 2.0 * poisson))
shear = 0.5 / (1.0 + poisson)

MASS = (0.25, 1.0 / 12.0)
MODES = [(mx, my, mz) for mx in (0, 1) for my in (0, 1) for mz in (0, 1)]


def mode_couplings():
    rows = {(c, m): [] for c in range(3) for m in MODES}
    for c in range(3):
        for m in MODES:
            own = 0.0
            for axis in range(3):
                if m[axis] == 1:
                    factor = lame + 2.0 * shear if axis == c else shear
                    others = [MASS[m[o]] for o in range(3) if o != axis]
                    own += factor * others[0] * others[1]
            if own:
                rows[c, m].append((own, c, m))
            for k in range(3):
                if k == c:
                    continue
                rest = 3 - c - k
                if m[c] == 1 and m[k] == 0:
                    factor = lame
                elif m[c] == 0 and m[k] == 1:
                    factor = shear
                else:
                    continue
                partner = list(m)
                partner[c], partner[k] = m[k], m[c]
                rows[c, m].append((factor * 0.25 * MASS[m[rest]], k, tuple(partner)))
    return rows


COUPLINGS = mode_couplings()
CORNER_DIAGONAL = sum(w for m in MODES for w, c, _ in COUPLINGS[0, m] if c == 0)


def kernel(
    shape,
    load_hbm, classes_hbm, densities_hbm,
    displacement_ref, residual_ref, direction_ref,
    load_v, classes_v, table_v, cells_v,
    S, ZL, ZU, YH, YLO, YL, YU, CLL, CLU, CUL, CUU,
    A, G, XT, TL, TR, XM, IM, INV, FZ, FYS, FY, FYZ, FXS, FX,
    RA, RB, RC, rows_v,
    in_sem, y_send, y_recv, x_send, x_recv, f_send, f_recv, a_send, a_recv,
):
    NGX, NGY, NGZ = shape
    ring = NGX // 2 * NGZ
    reach = ring // 4
    gx, gy, gz = (lax.axis_index(a) for a in ("gx", "gy", "gz"))
    core = lax.rem(gx, 2)
    along = lax.div(gx, 2) * NGZ + gz
    has = {
        ("z", -1): gz > 0, ("z", 1): gz < NGZ - 1,
        ("y", -1): gy > 0, ("y", 1): gy < NGY - 1,
        ("x", -1): gx > 0, ("x", 1): gx < NGX - 1,
    }

    def both(dy, dz):
        terms = []
        if dy:
            terms.append(has["y", dy])
        if dz:
            terms.append(has["z", dz])
        return terms[0] if len(terms) == 1 else jnp.logical_and(terms[0], terms[1])

    def ring_device(offset, flip):
        q = lax.rem(along + offset + ring, ring)
        c = 1 - core if flip else core
        return {"gx": lax.div(q, NGZ) * 2 + c, "gy": gy, "gz": lax.rem(q, NGZ)}

    def row_device(offset):
        return {"gx": gx, "gy": lax.rem(gy + offset, NGY), "gz": gz}

    def block_device(dx, dy, dz):
        return {"gx": gx + dx, "gy": gy + dy, "gz": gz + dz}

    window = [o for o in range(-(reach - 1), reach + 1) if o != 0]
    sides = [(dy, dz) for dy in (-1, 0, 1) for dz in (-1, 0, 1) if (dy, dz) != (0, 0)]
    side_buffer = {
        (0, -1): ZL, (0, 1): ZU, (-1, 0): YL, (1, 0): YU,
        (-1, -1): CLL, (-1, 1): CLU, (1, -1): CUL, (1, 1): CUU,
    }

    for (dy, dz), buffer in side_buffer.items():
        @pl.when(jnp.logical_not(both(dy, dz)))
        def _(buffer=buffer):
            buffer[...] = jnp.zeros_like(buffer)
    for dx, buffer in ((-1, TL), (1, TR)):
        @pl.when(jnp.logical_not(has["x", dx]))
        def _(buffer=buffer):
            buffer[...] = jnp.zeros_like(buffer)

    barrier = pltpu.get_barrier_semaphore()

    def tell(device):
        pl.semaphore_signal(barrier, inc=1, device_id=device, device_id_type=MESH)

    awaited = jnp.int32(0)
    for offset in (-reach, reach):
        for flip in (False, True):
            tell(ring_device(offset, flip))
            awaited = awaited + 1
    for dx in (-1, 1):
        @pl.when(has["x", dx])
        def _(dx=dx):
            tell(block_device(dx, 0, 0))
        awaited = awaited + has["x", dx].astype(jnp.int32)
    for offset in sorted(window, key=lambda o: -abs(o)):
        if abs(offset) != reach:
            tell(ring_device(-offset, False))
            awaited = awaited + 1
    for offset in range(1, NGY):
        tell(row_device(offset))
        awaited = awaited + 1
    for dy, dz in sides:
        if True:
            @pl.when(both(dy, dz))
            def _(dy=dy, dz=dz):
                tell(block_device(0, dy, dz))
            awaited = awaited + both(dy, dz).astype(jnp.int32)

    loads = [
        pltpu.make_async_copy(classes_hbm, classes_v, in_sem.at[0]),
        pltpu.make_async_copy(densities_hbm, table_v.at[:, pl.ds(0, 128)], in_sem.at[1]),
        pltpu.make_async_copy(load_hbm, load_v, in_sem.at[2]),
    ]
    for copy in loads:
        copy.start()

    lane = lax.broadcasted_iota(jnp.int32, (8, 128), 1)
    sub = lax.broadcasted_iota(jnp.int32, (8, 128), 0)
    lane1 = lax.broadcasted_iota(jnp.int32, (1, 128), 1)
    third, third1 = lax.div(lane, 3), lax.div(lane1, 3)

    def roll(v, shift, axis):
        return pltpu.roll(v, shift % v.shape[axis], axis)

    cells_v[...] = jnp.zeros_like(cells_v)
    loads[0].wait()
    cells_v[:, 0:7, 0:127] = classes_v[...]
    loads[1].wait()
    rho = table_v[...]
    table = jnp.broadcast_to(soft_floor + rho * rho * rho * (1.0 - soft_floor), (8, 128))
    inside = jnp.logical_and(sub < 7, lane < 127)
    previous = jnp.zeros((8, 128), jnp.float32)
    for z in range(8):
        if z < 7:
            picked = jnp.take_along_axis(table, cells_v[z], axis=1, mode="promise_in_bounds")
            s = jnp.where(inside, picked, 0.0)
        else:
            s = jnp.zeros((8, 128), jnp.float32)
        S[z, 4] = s
        s = s + roll(s, 1, 1)
        s = s + roll(s, 1, 0)
        S[z, 3] = s + previous
        previous = s
    loads[2].wait()
    for z in range(8):
        for c in range(3):
            S[z, c] = load_v[c, z]
    for f in range(4):
        YH[f] = jnp.concatenate([S[z, f, 7:8, :] for z in range(8)], axis=0)
        YLO[f] = jnp.concatenate([S[z, f, 0:1, :] for z in range(8)], axis=0)
        YLO[4 + f] = jnp.concatenate([S[z, f, 1:2, :] for z in range(8)], axis=0)
    YLO[8] = jnp.concatenate([S[z, 4, 0:1, :] for z in range(8)], axis=0)

    pl.semaphore_wait(barrier, awaited)

    def remote(source, target, sends, recvs, index, device):
        return pltpu.make_async_remote_copy(
            src_ref=source, dst_ref=target, send_sem=sends.at[index], recv_sem=recvs.at[index],
            device_id=device, device_id_type=MESH,
        )

    source_of = {
        (0, -1): S.at[pl.ds(0, 2)],
        (0, 1): S.at[7, pl.ds(0, 4)],
        (-1, 0): YLO,
        (1, 0): YH,
        (-1, -1): YLO.at[:, pl.ds(0, 2)],
        (-1, 1): YLO.at[pl.ds(0, 8), pl.ds(7, 1)],
        (1, -1): YH.at[:, pl.ds(0, 2)],
        (1, 1): YH.at[:, pl.ds(7, 1)],
    }
    y_copies = {
        (dy, dz): remote(source_of[dy, dz], side_buffer[-dy, -dz], y_send, y_recv, sides.index((dy, dz)), block_device(0, dy, dz))
        for dy, dz in sides
    }
    for dy, dz in sorted(sides, key=lambda side: -abs(side[0]) - abs(side[1])):
        @pl.when(both(dy, dz))
        def _(copy=y_copies[dy, dz]):
            copy.start()
    for dy, dz in sides:
        @pl.when(both(dy, dz))
        def _(copy=y_copies[-dy, -dz]):
            copy.wait_recv()

    def wide(tile):
        return jnp.broadcast_to(tile, (8, 128))

    top, bottom = sub == 0, sub == 7
    for f in range(4):
        low = YL[f] + jnp.where(top, wide(CLL[f]), 0.0) + jnp.where(bottom, wide(CLU[f, 0:1]), 0.0)
        low8 = CLU[f, 1:2]
        high = YU[f] + jnp.where(top, wide(CUL[f]), 0.0) + jnp.where(bottom, wide(CUU[f, 0:1]), 0.0)
        high8 = CUU[f, 1:2]
        G[f, 0:8] = YU[4 + f] + jnp.where(top, wide(CUL[4 + f]), 0.0) + jnp.where(bottom, wide(CUU[4 + f, 0:1]), 0.0)
        G[f, 8:9] = CUU[4 + f, 1:2]
        for z in range(9):
            tile = S[z, f] if z < 8 else ZU[1, f]
            if z == 0:
                tile = tile + ZL[f]
            if z == 7:
                tile = tile + ZU[0, f]
            lower = low[z : z + 1] if z < 8 else low8
            upper = high[z : z + 1] if z < 8 else high8
            A[z, f] = tile + jnp.where(top, wide(lower), 0.0) + jnp.where(bottom, wide(upper), 0.0)
    edge = YU[8]
    for z in range(8):
        tile = S[z, 4] if z < 7 else ZU[0, 4]
        row = edge[z : z + 1] if z < 7 else CUU[8, 0:1]
        A[z, 4] = jnp.where(bottom, wide(row), tile)

    packed = jnp.zeros((8, 128), jnp.float32)
    for f in range(4):
        for z in range(9):
            k = 9 * f + z
            packed = jnp.where(third == k, roll(A[z, f], 3 * k - 127, 1), packed)
        packed = jnp.where(third == 36 + f, roll(G[f, 0:8], 3 * (36 + f) - 127, 1), packed)
    for z in range(8):
        packed = jnp.where(lane == 120 + z, roll(A[z, 4], 120 + z, 1), packed)
    XT[0:8] = packed
    packed8 = jnp.zeros((1, 128), jnp.float32)
    for f in range(4):
        packed8 = jnp.where(third1 == f, roll(G[f, 8:9], 3 * f - 127, 1), packed8)
    XT[8:9] = packed8
    XT[9:16] = jnp.zeros((7, 128), jnp.float32)

    to_right = remote(XT, TL, x_send, x_recv, 0, block_device(1, 0, 0))
    to_left = remote(XT, TR, x_send, x_recv, 1, block_device(-1, 0, 0))

    @pl.when(has["x", 1])
    def _():
        to_right.start()

    @pl.when(has["x", -1])
    def _():
        to_left.start()

    @pl.when(has["x", -1])
    def _():
        to_right.wait_recv()

    @pl.when(has["x", 1])
    def _():
        to_left.wait_recv()

    def merged(left, right, lanes):
        return jnp.where(lax.rem(lanes, 3) == 2, roll(left, 2, 1), right)

    left_tile, right_tile = TL[0:8], TR[0:8]
    left_row, right_row = TL[8:9], TR[8:9]
    tile_in = merged(left_tile, right_tile, lane)
    row_in = merged(left_row, right_row, lane1)
    ends = jnp.logical_or(lane == 0, lane == 127)
    ends1 = jnp.logical_or(lane1 == 0, lane1 == 127)
    keep = jnp.logical_or(lane > 0, gx > 0)
    keep1 = jnp.logical_or(lane1 > 0, gx > 0)

    def inverse(d):
        return 1.0 / jnp.where(d > 0.0, d * CORNER_DIAGONAL, 1.0)

    d_tile = jnp.where(lane < 27, roll(right_tile, -81, 1), jnp.where(lane < 54, roll(right_tile, -54, 1), roll(right_tile, -27, 1)))
    d_side = jnp.where(third == 36, roll(right_tile, -9, 1), jnp.where(third == 37, roll(right_tile, -6, 1), roll(right_tile, -3, 1)))
    past = right_tile * inverse(jnp.where(lane >= 108, d_side, d_tile))
    d_row = jnp.where(third1 == 0, roll(right_row, -9, 1), jnp.where(third1 == 1, roll(right_row, -6, 1), roll(right_row, -3, 1)))
    past_row = right_row * inverse(d_row)

    def start_tile(value, incoming, k, ends_, keep_):
        value = value + jnp.where(ends_, roll(incoming, 126 - 3 * k, 1), 0.0)
        return jnp.where(keep_, value, 0.0)

    def shifted(p, incoming, k):
        lanes = lax.broadcasted_iota(jnp.int32, p.shape, 1)
        return jnp.where(lanes == 127, roll(incoming, 125 - 3 * k, 1), roll(p, -1, 1))

    inv_side = inverse(start_tile(G[3, 0:8], tile_in, 39, ends, keep))
    inv_corner = inverse(start_tile(G[3, 8:9], row_in, 3, ends1, keep1))
    side, corner = [], []
    for c in range(3):
        p = start_tile(G[c, 0:8], tile_in, 36 + c, ends, keep) * inv_side
        q = shifted(p, past, 36 + c)
        side.append((p + q, q - p))
        p = start_tile(G[c, 8:9], row_in, c, ends1, keep1) * inv_corner
        q = shifted(p, past_row, c)
        corner.append((p + q, q - p))
    owned = jnp.logical_and(jnp.logical_or(lane > 0, gx == 0), jnp.logical_or(sub > 0, gy == 0))
    rz = jnp.zeros((8, 128), jnp.float32)
    for z in range(9):
        inv = inverse(start_tile(A[z, 3], tile_in, 27 + z, ends, keep))
        INV[z] = inv
        for c in range(3):
            start = start_tile(A[z, c], tile_in, 9 * c + z, ends, keep)
            p = start * inv
            if z < 8:
                A[z, c] = start
                rz_mask = jnp.logical_and(owned, gz == 0) if z == 0 else owned
                rz = rz + jnp.where(rz_mask, start * p, 0.0)
            q = shifted(p, past, 9 * c + z)
            sums = (p + q, q - p)
            for m in range(2):
                XM[z, c, m, 0:8] = sums[m]
                XM[z, c, m, 8:9] = side[c][m][z : z + 1] if z < 8 else corner[c][m]

    def plane_modes(z):
        modes = {}
        for c in range(3):
            for mx in range(2):
                here, above = XM[z, c, mx, 0:8], XM[z, c, mx, 1:9]
                modes[c, mx, 0] = here + above
                modes[c, mx, 1] = above - here
        return modes

    def spread(first, second, axis, mask):
        return first - second + jnp.where(mask, roll(first + second, 1, axis), 0.0)

    def to_nodes(plane):
        tiles = []
        for c in range(3):
            rows = [spread(plane[c, mx, 0], plane[c, mx, 1], 0, sub > 0) for mx in range(2)]
            tiles.append(spread(rows[0], rows[1], 1, lane > 0))
        return tiles

    curvature = jnp.zeros((8, 128), jnp.float32)
    square = jnp.zeros((8, 128), jnp.float32)
    lower = plane_modes(0)
    carried = None
    for z in range(8):
        upper = plane_modes(z + 1)
        u = {}
        for key in lower:
            u[key + (0,)] = lower[key] + upper[key]
            u[key + (1,)] = upper[key] - lower[key]
        s = A[z, 4]
        if z < 7 or True:
            s = jnp.where(lane == 127, roll(right_tile, 7 - z, 1), s)
        f = {}
        for c in range(3):
            for m in MODES:
                total = None
                for weight, k, partner in COUPLINGS[c, m]:
                    term = u[(k,) + partner] * weight
                    total = term if total is None else total + term
                f[(c,) + m] = None if total is None else total * s
        plane, carry = {}, {}
        for c in range(3):
            for mx in range(2):
                for my in range(2):
                    first, second = f[c, mx, my, 0], f[c, mx, my, 1]
                    if first is None:
                        plane[c, mx, my], carry[c, mx, my] = -second, second
                    else:
                        plane[c, mx, my], carry[c, mx, my] = first - second, first + second
        if carried is not None:
            plane = {key: plane[key] + carried[key] for key in plane}
        carried = carry
        lower = upper
        inv = INV[z]
        mask = jnp.logical_and(owned, gz == 0) if z == 0 else owned
        for c, image in enumerate(to_nodes(plane)):
            image = jnp.where(keep, image, 0.0)
            IM[z, c] = image
            scaled = image * inv
            curvature = curvature + jnp.where(mask, A[z, c] * scaled, 0.0)
            square = square + jnp.where(mask, image * scaled, 0.0)

    def total_of(tile):
        return jnp.sum(jnp.sum(tile, axis=0, keepdims=True), axis=1, keepdims=True)

    row = jnp.where(lane1 == 0, total_of(rz), jnp.where(lane1 == 1, total_of(curvature), total_of(square)))

    rows_v[0:1] = row
    RA[0:1] = row
    for k in range(1, NGY):
        remote(rows_v.at[pl.ds(0, 1)], RA.at[pl.ds(k, 1)], a_send, a_recv, 0, row_device(k)).start()

    for c in range(3):
        FYS[c] = jnp.concatenate([IM[z, c, 7:8, :] for z in range(8)], axis=0)
    z_fix = remote(IM.at[7], FZ, f_send, f_recv, 0, block_device(0, 0, 1))
    y_fix = remote(FYS, FY, f_send, f_recv, 1, block_device(0, 1, 0))
    yz_fix = remote(FYS.at[:, pl.ds(7, 1)], FYZ, f_send, f_recv, 2, block_device(0, 1, 1))
    for copy, dy, dz in ((yz_fix, 1, 1), (y_fix, 1, 0), (z_fix, 0, 1)):
        @pl.when(both(dy, dz))
        def _(copy=copy):
            copy.start()

    def drain(ref, count, semaphore):
        block = ref.at[pl.ds(0, count)]
        pltpu.make_async_copy(block, block, semaphore).wait()

    drain(RA, NGY - 1, a_recv.at[0])
    row = jnp.sum(RA[...], axis=0, keepdims=True)
    rows_v[1:2] = row
    RB[0:1] = row
    for k, offset in enumerate(window):
        remote(rows_v.at[pl.ds(1, 1)], RB.at[pl.ds(k + 1, 1)], a_send, a_recv, 1, ring_device(offset, False)).start()

    for copy, dy, dz in ((z_fix, 0, -1), (y_fix, -1, 0), (yz_fix, -1, -1)):
        @pl.when(both(dy, dz))
        def _(copy=copy):
            copy.wait_recv()

    @pl.when(both(1, 0))
    def _():
        y_fix.wait_send()

    @pl.when(both(0, 1))
    def _():
        z_fix.wait_send()

    @pl.when(both(1, 1))
    def _():
        yz_fix.wait_send()

    @pl.when(has["z", -1])
    def _():
        IM[0] = FZ[...]

    @pl.when(has["y", -1])
    def _():
        for c in range(3):
            for z in range(8):
                IM[z, c, 0:1, :] = FY[c, z : z + 1, :]

    @pl.when(both(-1, -1))
    def _():
        for c in range(3):
            IM[0, c, 0:1, :] = FYZ[c]

    packed = jnp.zeros((8, 128), jnp.float32)
    for c in range(3):
        for z in range(8):
            k = 8 * c + z
            packed = jnp.where(lane == k, roll(IM[z, c], k - 127, 1), packed)
    FXS[...] = packed
    x_fix = remote(FXS, FX, f_send, f_recv, 3, block_device(1, 0, 0))

    @pl.when(has["x", 1])
    def _():
        x_fix.start()

    drain(RB, len(window), a_recv.at[1])
    row = jnp.sum(RB[...], axis=0, keepdims=True)
    rows_v[2:3] = row
    for k, (offset, flip) in enumerate(((-reach, False), (-reach, True), (reach, False), (reach, True))):
        remote(rows_v.at[pl.ds(2, 1)], RC.at[pl.ds(k, 1)], a_send, a_recv, 2, ring_device(offset, flip)).start()

    for dy, dz in sides:
        @pl.when(both(dy, dz))
        def _(copy=y_copies[dy, dz]):
            copy.wait_send()

    @pl.when(has["x", 1])
    def _():
        to_right.wait_send()
        x_fix.wait_send()

    @pl.when(has["x", -1])
    def _():
        to_left.wait_send()
        x_fix.wait_recv()
        fixed = FX[...]
        for c in range(3):
            for z in range(8):
                IM[z, c] = jnp.where(lane == 0, roll(fixed, -(8 * c + z), 1), IM[z, c])

    drain(RA, NGY - 1, a_send.at[0])
    drain(RB, len(window), a_send.at[1])
    drain(RC, 4, a_recv.at[2])
    row = jnp.sum(RC[0:4], axis=0, keepdims=True)
    rz, curvature, square = (row[:, i : i + 1] for i in range(3))
    alpha = rz / curvature
    beta = alpha * alpha * square / rz - 1.0
    alpha, beta = wide(alpha), wide(beta)
    for z in range(8):
        inv = INV[z]
        for c in range(3):
            start = A[z, c]
            p = start * inv
            residual = start - alpha * IM[z, c]
            displacement_ref[c, z] = alpha * p
            residual_ref[c, z] = residual
            direction_ref[c, z] = residual * inv + beta * p
    drain(RC, 4, a_send.at[2])


def on_device(shape, load, classes, densities):
    f32, i32 = jnp.float32, jnp.int32
    ring = shape[0] // 2 * shape[2]
    count_b = 2 * (ring // 4)
    dma = pltpu.SemaphoreType.DMA

    def rows(n):
        return pltpu.VMEM((-(-n // 8) * 8, 128), f32)

    table = jnp.pad(densities, (0, 64)).reshape(1, 128)
    out = jax.ShapeDtypeStruct(load.shape, f32)
    return pl.pallas_call(
        functools.partial(kernel, shape),
        out_shape=(out, out, out),
        in_specs=[pl.BlockSpec(memory_space=pl.ANY)] * 3,
        out_specs=(pl.BlockSpec(memory_space=pltpu.VMEM),) * 3,
        scratch_shapes=[
            pltpu.VMEM(load.shape, f32), pltpu.VMEM(classes.shape, i32), pltpu.VMEM((1, 128), f32), pltpu.VMEM((7, 8, 128), i32),
            pltpu.VMEM((8, 5, 8, 128), f32), pltpu.VMEM((4, 8, 128), f32), pltpu.VMEM((2, 5, 8, 128), f32),
            pltpu.VMEM((4, 8, 128), f32), pltpu.VMEM((9, 8, 128), f32), pltpu.VMEM((4, 8, 128), f32), pltpu.VMEM((9, 8, 128), f32),
            pltpu.VMEM((4, 1, 128), f32), pltpu.VMEM((4, 2, 128), f32), pltpu.VMEM((8, 1, 128), f32), pltpu.VMEM((9, 2, 128), f32),
            pltpu.VMEM((9, 5, 8, 128), f32), pltpu.VMEM((4, 16, 128), f32),
            pltpu.VMEM((16, 128), f32), pltpu.VMEM((16, 128), f32), pltpu.VMEM((16, 128), f32),
            pltpu.VMEM((9, 3, 2, 16, 128), f32), pltpu.VMEM((8, 3, 8, 128), f32), pltpu.VMEM((9, 8, 128), f32),
            pltpu.VMEM((3, 8, 128), f32), pltpu.VMEM((3, 8, 128), f32), pltpu.VMEM((3, 8, 128), f32), pltpu.VMEM((3, 1, 128), f32),
            pltpu.VMEM((8, 128), f32), pltpu.VMEM((8, 128), f32),
            pltpu.VMEM((shape[1], 128), f32), pltpu.VMEM((count_b, 128), f32), rows(4), rows(3),
            dma((3,)), dma((8,)), dma((8,)), dma((2,)), dma((2,)), dma((4,)), dma((4,)), dma((3,)), dma((3,)),
        ],
        compiler_params=pltpu.CompilerParams(collective_id=0, has_side_effects=True),
        name="step",
    )(load, classes, table)


def solution(mesh):
    shape = tuple(mesh.shape[a] for a in ("gx", "gy", "gz"))
    spec = P(None, "gz", "gy", "gx")
    return jax.shard_map(
        functools.partial(on_device, shape), mesh=mesh,
        in_specs=(spec, P("gz", "gy", "gx"), P()), out_specs=(spec, spec, spec), check_vma=False,
    )
```

```python
import functools
import math

import jax
import jax.numpy as jnp
import numpy as np
from jax import lax
from jax.experimental import pallas as pl
from jax.experimental.pallas import tpu as pltpu
from jax.sharding import PartitionSpec as P

MESH = pl.DeviceIdType.MESH
soft_floor = 0.001
poisson = 0.3
lame = poisson / ((1.0 + poisson) * (1.0 - 2.0 * poisson))
shear = 0.5 / (1.0 + poisson)

MASS = (0.25, 1.0 / 12.0)
MODES = [(mx, my, mz) for mx in (0, 1) for my in (0, 1) for mz in (0, 1)]


def mode_couplings():
    rows = {(c, m): [] for c in range(3) for m in MODES}
    for c in range(3):
        for m in MODES:
            own = 0.0
            for axis in range(3):
                if m[axis] == 1:
                    factor = lame + 2.0 * shear if axis == c else shear
                    others = [MASS[m[o]] for o in range(3) if o != axis]
                    own += factor * others[0] * others[1]
            if own:
                rows[c, m].append((own, c, m))
            for k in range(3):
                if k == c:
                    continue
                rest = 3 - c - k
                if m[c] == 1 and m[k] == 0:
                    factor = lame
                elif m[c] == 0 and m[k] == 1:
                    factor = shear
                else:
                    continue
                partner = list(m)
                partner[c], partner[k] = m[k], m[c]
                rows[c, m].append((factor * 0.25 * MASS[m[rest]], k, tuple(partner)))
    return rows


COUPLINGS = mode_couplings()
CORNER_DIAGONAL = sum(w for m in MODES for w, c, _ in COUPLINGS[0, m] if c == 0)


def apply_modes(u, s):
    out = {}
    for c in range(3):
        for m in MODES:
            total = None
            for weight, k, partner in COUPLINGS[c, m]:
                term = u[(k,) + partner] * weight
                total = term if total is None else total + term
            out[(c,) + m] = None if total is None else total * s
    return out


def roll(v, shift, axis):
    return pltpu.roll(v, shift % v.shape[axis], axis)


def inverse(d):
    return 1.0 / jnp.where(d > 0.0, d * CORNER_DIAGONAL, 1.0)


def wide(tile):
    return jnp.broadcast_to(tile, (8, 128))


def total_of(tile):
    return jnp.sum(jnp.sum(tile, axis=0, keepdims=True), axis=1, keepdims=True)


def strip_sums(lower, upper, counted):
    lane = lax.broadcasted_iota(jnp.int32, (16, 128), 1)
    first = lane < 64
    place = lax.rem(lane, 64)
    column, layer = lax.rem(place, 3), lax.div(place, 3)

    def shared(v):
        joined = v + jnp.where(first, roll(v, -62, 1), roll(v, 62, 1))
        return jnp.where(column == jnp.where(first, 2, 0), joined, v)

    def field(f):
        return jnp.where(first, roll(lower, -27 * f, 1), roll(upper, 61 - 27 * f, 1))

    s = jnp.zeros((16, 128), jnp.float32)
    row = lax.broadcasted_iota(jnp.int32, (16, 128), 0)
    for z in range(8):
        found = jnp.where(first, roll(lower, z - 108, 1), roll(upper, z - 111 + 64, 1))
        s = jnp.where(jnp.logical_and(layer == z, column < 2), found, s)
    s = jnp.where(row < 8, s, 0.0)
    d = shared(field(3))
    inv = inverse(d)
    starts, vectors, u = [], [], {}
    for c in range(3):
        start = shared(field(c))
        p = start * inv
        starts.append(start)
        vectors.append(p)
        q = roll(p, -1, 1)
        for mx, along_x in enumerate((p + q, q - p)):
            q = roll(along_x, -1, 0)
            for my, along_y in enumerate((along_x + q, q - along_x)):
                q = roll(along_y, -3, 1)
                u[c, mx, my, 0] = along_y + q
                u[c, mx, my, 1] = q - along_y
    f = apply_modes(u, s)
    rz = curvature = square = jnp.zeros((16, 128), jnp.float32)
    parts = []

    def back(a, b, shift, axis):
        low, high = (-b, b) if a is None else (a - b, a + b)
        return low + roll(high, shift, axis)

    for c in range(3):
        x_parts = []
        for mx in range(2):
            y_parts = [back(f[c, mx, my, 0], f[c, mx, my, 1], 3, 1) for my in range(2)]
            x_parts.append(back(y_parts[0], y_parts[1], 1, 0))
        image = shared(back(x_parts[0], x_parts[1], 1, 1))
        scaled = image * inv
        rz = rz + jnp.where(counted, starts[c] * vectors[c], 0.0)
        curvature = curvature + jnp.where(counted, vectors[c] * image, 0.0)
        square = square + jnp.where(counted, image * scaled, 0.0)
        moved = jnp.where(first, roll(starts[c], -2, 1), roll(starts[c], 2, 1))
        parts.append(jnp.where(column == jnp.where(first, 0, 2), moved, image)[0:8])
    parts.append(d[0:8])
    lane8 = lane[0:8]
    for_lower = for_upper = jnp.zeros((8, 128), jnp.float32)
    for i, part in enumerate(parts):
        here = lax.div(lane8, 24) == i
        for_lower = jnp.where(here, roll(part, 24 * i, 1), for_lower)
        for_upper = jnp.where(here, roll(part, 24 * i - 64, 1), for_upper)
    return (rz, curvature, square), for_lower, for_upper


def kernel(
    shape,
    load_hbm, classes_hbm, densities_hbm,
    displacement_ref, residual_ref, direction_ref,
    load_v, classes_v, table_v, cells_v,
    S, ZL, ZU, YH, YLO, YL, YU, CLL, CLU, CUL, CUU,
    A, G, SL, SU, SR, XM, IM, INV, FZ, FYS, FY, FYZ, RS, LOW, HIGH,
    RA, RB, rows_v,
    in_sem, y_send, y_recv, x_send, x_recv, f_send, f_recv, a_send, a_recv, relay,
):
    NGX, NGY, NGZ = shape
    ring = NGX // 2 * NGZ
    gx, gy, gz = (lax.axis_index(a) for a in ("gx", "gy", "gz"))
    core = lax.rem(gx, 2)
    along = lax.div(gx, 2) * NGZ + gz
    pivot = NGX - 2
    mirrored = gx >= pivot
    has_face = jnp.logical_or(jnp.logical_and(mirrored, gx > 0), gx < pivot - 1)
    gives_left = jnp.logical_and(gx >= 1, gx <= pivot - 1)
    gives_right = jnp.logical_and(gx >= pivot - 1, gx <= NGX - 2)

    def both(dy, dz):
        terms = []
        if dy:
            terms.append(gy > 0 if dy < 0 else gy < NGY - 1)
        if dz:
            terms.append(gz > 0 if dz < 0 else gz < NGZ - 1)
        return terms[0] if len(terms) == 1 else jnp.logical_and(terms[0], terms[1])

    def ring_device(offset, flip=False):
        q = lax.rem(along + (offset % ring), ring)
        c = 1 - core if flip else core
        return {"gx": lax.div(q, NGZ) * 2 + c, "gy": gy, "gz": lax.rem(q, NGZ)}

    def row_device(offset, flip=False):
        c = 1 - core if flip else core
        return {"gx": gx - core + c, "gy": lax.rem(gy + offset, NGY), "gz": gz}

    def plane_device(dy, dx):
        y, x = lax.rem(lax.div(gy, 4) + dy, 4), lax.rem(lax.rem(gy, 4) + dx, 4)
        return {"gx": gx, "gy": y * 4 + x, "gz": gz}

    def block_device(dx, dy, dz):
        return {"gx": gx + dx, "gy": gy + dy, "gz": gz + dz}

    sides = [(dy, dz) for dy in (-1, 0, 1) for dz in (-1, 0, 1) if (dy, dz) != (0, 0)]
    side_buffer = {
        (0, -1): ZL, (0, 1): ZU, (-1, 0): YL, (1, 0): YU,
        (-1, -1): CLL, (-1, 1): CLU, (1, -1): CUL, (1, 1): CUU,
    }

    for (dy, dz), buffer in side_buffer.items():
        @pl.when(jnp.logical_not(both(dy, dz)))
        def _(buffer=buffer):
            buffer[...] = jnp.zeros_like(buffer)
    SR[...] = jnp.zeros_like(SR)

    barrier = pltpu.get_barrier_semaphore()

    def tell(device, semaphore):
        pl.semaphore_signal(semaphore, inc=1, device_id=device, device_id_type=MESH)

    near = [ring_device(o) for o in sorted({1, 2, ring - 1, ring - 2})]
    if NGY == 16:
        plane = [plane_device(*o) for o in ((0, 1), (0, 3), (1, 0), (3, 0))]
        plane_far = [plane_device(*o) for o in ((0, 2), (2, 0))]
    else:
        plane, plane_far = [row_device(o) for o in range(1, NGY)], []
    flipped = row_device(0, True)
    relays = [
        ([ring_device(o) for o in (2, -2)] if ring >= 8 else []) + plane,
        ([ring_device(o) for o in (4, -4)] if ring >= 16 else []) + plane_far,
        [flipped],
        [ring_device(o) for o in (8, -8)] if ring >= 32 else [],
    ]

    def relay_tell(step):
        for device in relays[step]:
            tell(device, relay.at[step])

    def relay_wait(step):
        if relays[step]:
            pl.semaphore_wait(relay.at[step], len(relays[step]))

    awaited = jnp.int32(0)
    for dy, dz in sorted(sides, key=lambda side: -abs(side[0]) - abs(side[1])):
        @pl.when(both(dy, dz))
        def _(dy=dy, dz=dz):
            tell(block_device(0, dy, dz), barrier)
        awaited = awaited + both(dy, dz).astype(jnp.int32)
    for device in near + plane + [flipped]:
        tell(device, barrier)
        awaited = awaited + 1

    @pl.when(jnp.logical_and(gx < pivot - 1, core == 1))
    def _():
        tell(block_device(1, 0, 0), barrier)
    awaited = awaited + jnp.logical_and(gives_left, core == 0).astype(jnp.int32)

    loads = [
        pltpu.make_async_copy(classes_hbm, classes_v, in_sem.at[0]),
        pltpu.make_async_copy(densities_hbm, table_v, in_sem.at[1]),
        pltpu.make_async_copy(load_hbm, load_v, in_sem.at[2]),
    ]
    for copy in loads:
        copy.start()

    lane = lax.broadcasted_iota(jnp.int32, (8, 128), 1)
    sub = lax.broadcasted_iota(jnp.int32, (8, 128), 0)
    lane1 = lax.broadcasted_iota(jnp.int32, (1, 128), 1)
    third, third1 = lax.div(lane, 3), lax.div(lane1, 3)

    cells_v[...] = jnp.zeros_like(cells_v)
    loads[0].wait()
    cells_v[:, 0:7, 0:127] = classes_v[...]
    loads[1].wait()
    rho = table_v[...]
    rho = jnp.concatenate([rho, rho], axis=1)
    table = wide(soft_floor + rho * rho * rho * (1.0 - soft_floor))
    inside = jnp.logical_and(sub < 7, lane < 127)
    previous = jnp.zeros((8, 128), jnp.float32)
    for z in range(8):
        if z < 7:
            picked = jnp.take_along_axis(table, cells_v[z], axis=1, mode="promise_in_bounds")
            s = jnp.where(inside, picked, 0.0)
        else:
            s = jnp.zeros((8, 128), jnp.float32)
        S[z, 4] = s
        s = s + roll(s, 1, 1)
        s = s + roll(s, 1, 0)
        S[z, 3] = s + previous
        previous = s
    loads[2].wait()
    for z in range(8):
        for c in range(3):
            S[z, c] = load_v[c, z]
    for f in range(4):
        YH[f] = jnp.concatenate([S[z, f, 7:8, :] for z in range(8)], axis=0)
        YLO[f] = jnp.concatenate([S[z, f, 0:1, :] for z in range(8)], axis=0)
        YLO[4 + f] = jnp.concatenate([S[z, f, 1:2, :] for z in range(8)], axis=0)
    YLO[8] = jnp.concatenate([S[z, 4, 0:1, :] for z in range(8)], axis=0)

    pl.semaphore_wait(barrier, awaited)

    def remote(source, target, sends, recvs, index, device):
        return pltpu.make_async_remote_copy(
            src_ref=source, dst_ref=target, send_sem=sends.at[index], recv_sem=recvs.at[index],
            device_id=device, device_id_type=MESH,
        )

    source_of = {
        (0, -1): S.at[pl.ds(0, 2)],
        (0, 1): S.at[7, pl.ds(0, 4)],
        (-1, 0): YLO,
        (1, 0): YH,
        (-1, -1): YLO.at[:, pl.ds(0, 2)],
        (-1, 1): YLO.at[pl.ds(0, 8), pl.ds(7, 1)],
        (1, -1): YH.at[:, pl.ds(0, 2)],
        (1, 1): YH.at[:, pl.ds(7, 1)],
    }
    y_copies = {
        (dy, dz): remote(source_of[dy, dz], side_buffer[-dy, -dz], y_send, y_recv, sides.index((dy, dz)), block_device(0, dy, dz))
        for dy, dz in sides
    }
    for dy, dz in sorted(sides, key=lambda side: -abs(side[0]) - abs(side[1])):
        @pl.when(both(dy, dz))
        def _(copy=y_copies[dy, dz]):
            copy.start()
    relay_tell(0)
    relay_wait(0)
    relay_tell(1)
    for dy, dz in sides:
        @pl.when(both(dy, dz))
        def _(copy=y_copies[-dy, -dz]):
            copy.wait_recv()

    top, bottom = sub == 0, sub == 7
    for f in range(4):
        low = YL[f] + jnp.where(top, wide(CLL[f]), 0.0) + jnp.where(bottom, wide(CLU[f, 0:1]), 0.0)
        low8 = CLU[f, 1:2]
        high = YU[f] + jnp.where(top, wide(CUL[f]), 0.0) + jnp.where(bottom, wide(CUU[f, 0:1]), 0.0)
        high8 = CUU[f, 1:2]
        G[f, 0:8] = YU[4 + f] + jnp.where(top, wide(CUL[4 + f]), 0.0) + jnp.where(bottom, wide(CUU[4 + f, 0:1]), 0.0)
        G[f, 8:9] = CUU[4 + f, 1:2]
        for z in range(9):
            tile = S[z, f] if z < 8 else ZU[1, f]
            if z == 0:
                tile = tile + ZL[f]
            if z == 7:
                tile = tile + ZU[0, f]
            lower = low[z : z + 1] if z < 8 else low8
            upper = high[z : z + 1] if z < 8 else high8
            A[z, f] = tile + jnp.where(top, wide(lower), 0.0) + jnp.where(bottom, wide(upper), 0.0)
    edge = YU[8]
    for z in range(8):
        tile = S[z, 4] if z < 7 else ZU[0, 4]
        row = edge[z : z + 1] if z < 7 else CUU[8, 0:1]
        A[z, 4] = jnp.where(bottom, wide(row), tile)

    low_tile = high_tile = jnp.zeros((8, 128), jnp.float32)
    low_row = high_row = jnp.zeros((1, 128), jnp.float32)
    for f in range(4):
        for z in range(9):
            k = 9 * f + z
            tile = roll(A[z, f], 3 * k - 125, 1)
            high_tile = jnp.where(third == k, tile, high_tile)
            low_tile = jnp.where(third == k + 1, tile, low_tile)
            row = roll(G[f, z : z + 1], 3 * k - 125, 1)
            high_row = jnp.where(third1 == k, row, high_row)
            low_row = jnp.where(third1 == k + 1, row, low_row)
    for z in range(8):
        tile = roll(A[z, 4], 108 + 2 * z - 125, 1)
        high_tile = jnp.where(lax.div(lane - 108, 2) == z if z else jnp.logical_or(lane == 108, lane == 109), tile, high_tile)
        low_tile = jnp.where(lax.div(lane - 111, 2) == z if z else jnp.logical_or(lane == 111, lane == 112), tile, low_tile)
    for buffer, tile, row in ((SL, high_tile, high_row), (SU, low_tile, low_row)):
        buffer[0:8] = tile
        buffer[8:9] = row
        buffer[9:16] = jnp.zeros((7, 128), jnp.float32)

    nine = pl.ds(0, 9)
    to_left = remote(SU.at[nine], SR.at[nine], x_send, x_recv, 0, block_device(-1, 0, 0))
    to_right = remote(SL.at[nine], SR.at[nine], x_send, x_recv, 1, block_device(1, 0, 0))

    @pl.when(gives_left)
    def _():
        to_left.start()

    relay_wait(1)
    relay_tell(2)
    relay_wait(2)

    @pl.when(gives_right)
    def _():
        to_right.start()

    relay_tell(3)

    keep = jnp.logical_or(lane > 0, gx > 0)
    keep1 = jnp.logical_or(lane1 > 0, gx > 0)
    inv_side = inverse(G[3, 0:8])
    inv_corner = inverse(G[3, 8:9])

    def along_x(p):
        q = roll(p, -1, 1)
        return p + q, q - p

    side = [along_x(jnp.where(keep, G[c, 0:8], 0.0) * inv_side) for c in range(3)]
    corner = [along_x(jnp.where(keep1, G[c, 8:9], 0.0) * inv_corner) for c in range(3)]
    owned = jnp.logical_and(
        jnp.logical_and(jnp.logical_or(lane > 1, gx == 0), jnp.logical_or(lane < 126, gx == NGX - 1)),
        jnp.logical_or(sub > 0, gy == 0),
    )
    owned_first = jnp.logical_and(owned, gz == 0)
    rz = jnp.zeros((8, 128), jnp.float32)
    for z in range(9):
        inv = inverse(A[z, 3])
        INV[z] = inv
        for c in range(3):
            start = jnp.where(keep, A[z, c], 0.0)
            p = start * inv
            if z < 8:
                A[z, c] = start
                rz = rz + jnp.where(owned if z else owned_first, start * p, 0.0)
            sums = along_x(p)
            for m in range(2):
                XM[z, c, m, 0:8] = sums[m]
                XM[z, c, m, 8:9] = side[c][m][z : z + 1] if z < 8 else corner[c][m]

    def plane_modes(z):
        modes = {}
        for c in range(3):
            for mx in range(2):
                here, above = XM[z, c, mx, 0:8], XM[z, c, mx, 1:9]
                modes[c, mx, 0] = here + above
                modes[c, mx, 1] = above - here
        return modes

    def spread(first, second, axis, mask):
        return first - second + jnp.where(mask, roll(first + second, 1, axis), 0.0)

    curvature = jnp.zeros((8, 128), jnp.float32)
    square = jnp.zeros((8, 128), jnp.float32)
    lower = plane_modes(0)
    carried = None
    for z in range(8):
        upper = plane_modes(z + 1)
        u = {}
        for key in lower:
            u[key + (0,)] = lower[key] + upper[key]
            u[key + (1,)] = upper[key] - lower[key]
        f = apply_modes(u, A[z, 4])
        here, carry = {}, {}
        for c in range(3):
            for mx in range(2):
                for my in range(2):
                    first, second = f[c, mx, my, 0], f[c, mx, my, 1]
                    if first is None:
                        here[c, mx, my], carry[c, mx, my] = -second, second
                    else:
                        here[c, mx, my], carry[c, mx, my] = first - second, first + second
        if carried is not None:
            here = {key: here[key] + carried[key] for key in here}
        carried = carry
        lower = upper
        inv = INV[z]
        mask = owned if z else owned_first
        for c in range(3):
            rows = [spread(here[c, mx, 0], here[c, mx, 1], 0, sub > 0) for mx in range(2)]
            image = jnp.where(keep, spread(rows[0], rows[1], 1, lane > 0), 0.0)
            IM[z, c] = image
            scaled = image * inv
            curvature = curvature + jnp.where(mask, A[z, c] * scaled, 0.0)
            square = square + jnp.where(mask, image * scaled, 0.0)

    @pl.when(jnp.logical_and(has_face, jnp.logical_not(mirrored)))
    def _():
        to_left.wait_recv()

    @pl.when(jnp.logical_and(has_face, mirrored))
    def _():
        to_right.wait_recv()

    lane16 = lax.broadcasted_iota(jnp.int32, (16, 128), 1)
    sub16 = lax.broadcasted_iota(jnp.int32, (16, 128), 0)
    place = lax.rem(lane16, 64)
    column, layer = lax.rem(place, 3), lax.div(place, 3)
    counted = jnp.logical_and(
        jnp.logical_and(
            jnp.logical_and(sub16 < 8, jnp.logical_or(sub16 > 0, gy == 0)),
            jnp.logical_and(layer < 8, jnp.logical_or(layer > 0, gz == 0)),
        ),
        jnp.logical_and(has_face, jnp.where(lane16 < 64, column, 2 - 2 * jnp.abs(column - 1)) > 0),
    )
    received = SR[...]
    sums, for_lower, for_upper = strip_sums(
        jnp.where(mirrored, received, SL[...]), jnp.where(mirrored, SU[...], received), counted
    )
    rz, curvature, square = (
        total_of(own + part[0:8] + part[8:16]) for own, part in zip((rz, curvature, square), sums)
    )

    row = jnp.where(lane1 == 0, rz, jnp.where(lane1 == 1, curvature, square))
    rows_v[0:1] = row
    RA[0:1] = row
    for flip in (True, False):
        for k in range(NGY):
            if k or flip:
                slot = k + (NGY if flip else 0)
                remote(rows_v.at[pl.ds(0, 1)], RA.at[pl.ds(slot, 1)], a_send, a_recv, 0, row_device(k, flip)).start()

    RS[0] = for_lower
    RS[1] = for_upper
    result_right = remote(RS.at[1], LOW, f_send, f_recv, 3, block_device(1, 0, 0))
    result_left = remote(RS.at[0], HIGH, f_send, f_recv, 4, block_device(-1, 0, 0))
    normal_face = jnp.logical_and(has_face, jnp.logical_not(mirrored))
    mirrored_face = jnp.logical_and(has_face, mirrored)

    @pl.when(normal_face)
    def _():
        result_right.start()
        HIGH[...] = for_lower

    @pl.when(mirrored_face)
    def _():
        result_left.start()
        LOW[...] = for_upper

    def drain(ref, count, semaphore):
        block = ref.at[pl.ds(0, count)]
        pltpu.make_async_copy(block, block, semaphore).wait()

    drain(RA, 2 * NGY - 1, a_recv.at[0])
    row = jnp.sum(RA[...], axis=0, keepdims=True)
    rows_v[1:2] = row
    RB[0:1] = row
    relay_wait(3)
    for k in sorted(range(1, ring), key=lambda k: -min(k, ring - k)):
        remote(rows_v.at[pl.ds(1, 1)], RB.at[pl.ds(k, 1)], a_send, a_recv, 1, ring_device(k)).start()

    @pl.when(gives_left)
    def _():
        result_right.wait_recv()

    @pl.when(jnp.logical_or(gives_left, mirrored_face))
    def _():
        tile = LOW[...]
        for z in range(8):
            diagonal = roll(tile, -(72 + 3 * z), 1)
            INV[z] = jnp.where(lane == 0, inverse(diagonal), INV[z])
            for c in range(3):
                k = 24 * c + 3 * z
                IM[z, c] = jnp.where(lane < 2, roll(tile, -k, 1), IM[z, c])
                A[z, c] = jnp.where(lane == 0, roll(tile, -(k + 2), 1), A[z, c])

    @pl.when(gives_right)
    def _():
        result_left.wait_recv()

    @pl.when(jnp.logical_or(gives_right, normal_face))
    def _():
        tile = HIGH[...]
        for z in range(8):
            diagonal = roll(tile, 127 - (72 + 3 * z + 2), 1)
            INV[z] = jnp.where(lane == 127, inverse(diagonal), INV[z])
            for c in range(3):
                k = 24 * c + 3 * z
                IM[z, c] = jnp.where(lane > 125, roll(tile, 127 - (k + 2), 1), IM[z, c])
                A[z, c] = jnp.where(lane == 127, roll(tile, 127 - k, 1), A[z, c])

    for c in range(3):
        FYS[c] = jnp.concatenate([IM[z, c, 7:8, :] for z in range(8)], axis=0)
    z_fix = remote(IM.at[7], FZ, f_send, f_recv, 0, block_device(0, 0, 1))
    y_fix = remote(FYS, FY, f_send, f_recv, 1, block_device(0, 1, 0))
    yz_fix = remote(FYS.at[:, pl.ds(7, 1)], FYZ, f_send, f_recv, 2, block_device(0, 1, 1))
    fixes = ((yz_fix, 1, 1), (y_fix, 1, 0), (z_fix, 0, 1))
    for copy, dy, dz in fixes:
        @pl.when(both(dy, dz))
        def _(copy=copy):
            copy.start()
    for dy, dz in sides:
        @pl.when(both(dy, dz))
        def _(copy=y_copies[dy, dz]):
            copy.wait_send()
    for copy, dy, dz in fixes:
        @pl.when(both(-dy, -dz))
        def _(copy=copy):
            copy.wait_recv()
    for copy, dy, dz in fixes:
        @pl.when(both(dy, dz))
        def _(copy=copy):
            copy.wait_send()

    @pl.when(gz > 0)
    def _():
        IM[0] = FZ[...]

    @pl.when(gy > 0)
    def _():
        for c in range(3):
            for z in range(8):
                IM[z, c, 0:1, :] = FY[c, z : z + 1, :]

    @pl.when(both(-1, -1))
    def _():
        for c in range(3):
            IM[0, c, 0:1, :] = FYZ[c]

    for copy, condition in (
        (to_left, gives_left), (to_right, gives_right), (result_right, normal_face), (result_left, mirrored_face),
    ):
        @pl.when(condition)
        def _(copy=copy):
            copy.wait_send()
    drain(RA, 2 * NGY - 1, a_send.at[0])
    drain(RB, ring - 1, a_recv.at[1])
    row = jnp.sum(RB[...], axis=0, keepdims=True)
    rz, curvature, square = (row[:, i : i + 1] for i in range(3))
    alpha = rz / curvature
    beta = alpha * alpha * square / rz - 1.0
    alpha, beta = wide(alpha), wide(beta)
    for z in range(8):
        inv = INV[z]
        for c in range(3):
            start = A[z, c]
            p = start * inv
            residual = start - alpha * IM[z, c]
            displacement_ref[c, z] = alpha * p
            residual_ref[c, z] = residual
            direction_ref[c, z] = residual * inv + beta * p
    drain(RB, ring - 1, a_send.at[1])


def store_kernel(a_ref, b_ref, c_ref, a_out, b_out, c_out, sem):
    copies = [
        pltpu.make_async_copy(source, target, sem.at[i])
        for i, (source, target) in enumerate(((a_ref, a_out), (b_ref, b_out), (c_ref, c_out)))
    ]
    for copy in copies:
        copy.start()
    for copy in copies:
        copy.wait()


def on_device(shape, load, classes, densities):
    f32, i32 = jnp.float32, jnp.int32
    ring = shape[0] // 2 * shape[2]
    dma = pltpu.SemaphoreType.DMA

    def rows(n):
        return pltpu.VMEM((n, 128), f32)

    def tiles(*dims):
        return pltpu.VMEM(dims + (8, 128), f32)

    out = jax.ShapeDtypeStruct(load.shape, f32)
    outs = pl.pallas_call(
        functools.partial(kernel, shape),
        out_shape=(out, out, out),
        in_specs=[pl.BlockSpec(memory_space=pl.ANY)] * 3,
        out_specs=(pl.BlockSpec(memory_space=pltpu.VMEM),) * 3,
        scratch_shapes=[
            pltpu.VMEM(load.shape, f32), pltpu.VMEM(classes.shape, i32), pltpu.VMEM((1, 64), f32), pltpu.VMEM((7, 8, 128), i32),
            tiles(8, 5), tiles(4), tiles(2, 5), tiles(4), tiles(9), tiles(4), tiles(9),
            pltpu.VMEM((4, 1, 128), f32), pltpu.VMEM((4, 2, 128), f32), pltpu.VMEM((8, 1, 128), f32), pltpu.VMEM((9, 2, 128), f32),
            tiles(9, 5), pltpu.VMEM((4, 16, 128), f32), rows(16), rows(16), rows(16),
            pltpu.VMEM((9, 3, 2, 16, 128), f32), tiles(8, 3), tiles(9),
            tiles(3), tiles(3), tiles(3), pltpu.VMEM((3, 1, 128), f32), tiles(2), tiles(), tiles(),
            rows(2 * shape[1]), rows(ring), rows(2),
            dma((3,)), dma((8,)), dma((8,)), dma((2,)), dma((2,)), dma((5,)), dma((5,)), dma((2,)), dma((2,)),
            pltpu.SemaphoreType.REGULAR((4,)),
        ],
        compiler_params=pltpu.CompilerParams(collective_id=0, has_side_effects=True),
        name="step",
    )(load, classes, densities.reshape(1, 64))
    return pl.pallas_call(
        store_kernel,
        out_shape=(out, out, out),
        in_specs=[pl.BlockSpec(memory_space=pltpu.VMEM)] * 3,
        out_specs=(pl.BlockSpec(memory_space=pl.ANY),) * 3,
        scratch_shapes=[dma((3,))],
        name="store",
    )(*outs)


def solution(mesh):
    shape = tuple(mesh.shape[a] for a in ("gx", "gy", "gz"))
    spec = P(None, "gz", "gy", "gx")
    return jax.shard_map(
        functools.partial(on_device, shape), mesh=mesh,
        in_specs=(spec, P("gz", "gy", "gx"), P()), out_specs=(spec, spec, spec), check_vma=False,
    )
```

```python
import functools
import math

import jax
import jax.numpy as jnp
import numpy as np
from jax import lax
from jax.experimental import pallas as pl
from jax.experimental.pallas import tpu as pltpu
from jax.sharding import PartitionSpec as P

MESH = pl.DeviceIdType.MESH
soft_floor = 0.001
poisson = 0.3
lame = poisson / ((1.0 + poisson) * (1.0 - 2.0 * poisson))
shear = 0.5 / (1.0 + poisson)

MASS = (0.25, 1.0 / 12.0)
MODES = [(mx, my, mz) for mx in (0, 1) for my in (0, 1) for mz in (0, 1)]


def mode_couplings():
    rows = {(c, m): [] for c in range(3) for m in MODES}
    for c in range(3):
        for m in MODES:
            own = 0.0
            for axis in range(3):
                if m[axis] == 1:
                    factor = lame + 2.0 * shear if axis == c else shear
                    others = [MASS[m[o]] for o in range(3) if o != axis]
                    own += factor * others[0] * others[1]
            if own:
                rows[c, m].append((own, c, m))
            for k in range(3):
                if k == c:
                    continue
                rest = 3 - c - k
                if m[c] == 1 and m[k] == 0:
                    factor = lame
                elif m[c] == 0 and m[k] == 1:
                    factor = shear
                else:
                    continue
                partner = list(m)
                partner[c], partner[k] = m[k], m[c]
                rows[c, m].append((factor * 0.25 * MASS[m[rest]], k, tuple(partner)))
    return rows


COUPLINGS = mode_couplings()
CORNER_DIAGONAL = sum(w for m in MODES for w, c, _ in COUPLINGS[0, m] if c == 0)


def apply_modes(u, s):
    out = {}
    for c in range(3):
        for m in MODES:
            total = None
            for weight, k, partner in COUPLINGS[c, m]:
                term = u[(k,) + partner] * weight
                total = term if total is None else total + term
            out[(c,) + m] = None if total is None else total * s
    return out


def roll(v, shift, axis):
    return pltpu.roll(v, shift % v.shape[axis], axis)


def inverse(d):
    return 1.0 / jnp.where(d > 0.0, d * CORNER_DIAGONAL, 1.0)


def wide(tile):
    return jnp.broadcast_to(tile, (8, 128))


def total_of(tile):
    return jnp.sum(jnp.sum(tile, axis=0, keepdims=True), axis=1, keepdims=True)


def strip_sums(lower, upper, counted):
    lane = lax.broadcasted_iota(jnp.int32, (16, 128), 1)
    first = lane < 64
    place = lax.rem(lane, 64)
    column, layer = lax.rem(place, 3), lax.div(place, 3)

    def shared(v):
        joined = v + jnp.where(first, roll(v, -62, 1), roll(v, 62, 1))
        return jnp.where(column == jnp.where(first, 2, 0), joined, v)

    def field(f):
        return jnp.where(first, roll(lower, -27 * f, 1), roll(upper, 61 - 27 * f, 1))

    s = jnp.zeros((16, 128), jnp.float32)
    row = lax.broadcasted_iota(jnp.int32, (16, 128), 0)
    for z in range(8):
        found = jnp.where(first, roll(lower, z - 108, 1), roll(upper, z - 111 + 64, 1))
        s = jnp.where(jnp.logical_and(layer == z, column < 2), found, s)
    s = jnp.where(row < 8, s, 0.0)
    d = shared(field(3))
    inv = inverse(d)
    starts, vectors, u = [], [], {}
    for c in range(3):
        start = shared(field(c))
        p = start * inv
        starts.append(start)
        vectors.append(p)
        q = roll(p, -1, 1)
        for mx, along_x in enumerate((p + q, q - p)):
            q = roll(along_x, -1, 0)
            for my, along_y in enumerate((along_x + q, q - along_x)):
                q = roll(along_y, -3, 1)
                u[c, mx, my, 0] = along_y + q
                u[c, mx, my, 1] = q - along_y
    f = apply_modes(u, s)
    rz = curvature = square = jnp.zeros((16, 128), jnp.float32)
    parts = []

    def back(a, b, shift, axis):
        low, high = (-b, b) if a is None else (a - b, a + b)
        return low + roll(high, shift, axis)

    for c in range(3):
        x_parts = []
        for mx in range(2):
            y_parts = [back(f[c, mx, my, 0], f[c, mx, my, 1], 3, 1) for my in range(2)]
            x_parts.append(back(y_parts[0], y_parts[1], 1, 0))
        image = shared(back(x_parts[0], x_parts[1], 1, 1))
        scaled = image * inv
        rz = rz + jnp.where(counted, starts[c] * vectors[c], 0.0)
        curvature = curvature + jnp.where(counted, vectors[c] * image, 0.0)
        square = square + jnp.where(counted, image * scaled, 0.0)
        moved = jnp.where(first, roll(starts[c], -2, 1), roll(starts[c], 2, 1))
        parts.append(jnp.where(column == jnp.where(first, 0, 2), moved, image)[0:8])
    parts.append(d[0:8])
    lane8 = lane[0:8]
    for_lower = for_upper = jnp.zeros((8, 128), jnp.float32)
    for i, part in enumerate(parts):
        here = lax.div(lane8, 24) == i
        for_lower = jnp.where(here, roll(part, 24 * i, 1), for_lower)
        for_upper = jnp.where(here, roll(part, 24 * i - 64, 1), for_upper)
    return (rz, curvature, square), for_lower, for_upper


def kernel(
    shape,
    load_hbm, classes_hbm, densities_hbm,
    displacement_ref, residual_ref, direction_ref,
    load_v, classes_v, table_v, cells_v,
    S, ZL, ZU, YH, YLO, YL, YU, CLL, CLU, CUL, CUU,
    A, G, SL, SU, SR, XM, IM, INV, FZ, FYS, FY, FYZ, RS, LOW, HIGH,
    RA, RB, rows_v,
    in_sem, y_send, y_recv, x_send, x_recv, f_send, f_recv, a_send, a_recv, relay,
):
    NGX, NGY, NGZ = shape
    ring = NGX // 2 * NGZ
    gx, gy, gz = (lax.axis_index(a) for a in ("gx", "gy", "gz"))
    core = lax.rem(gx, 2)
    along = lax.div(gx, 2) * NGZ + gz
    pivot = jnp.where(gz < 5 * NGZ // 8, NGX - 2, NGX - 4)
    mirrored = gx >= pivot
    has_face = jnp.logical_or(jnp.logical_and(mirrored, gx > 0), gx < pivot - 1)
    gives_left = jnp.logical_and(gx >= 1, gx <= pivot - 1)
    gives_right = jnp.logical_and(gx >= pivot - 1, gx <= NGX - 2)

    def both(dy, dz):
        terms = []
        if dy:
            terms.append(gy > 0 if dy < 0 else gy < NGY - 1)
        if dz:
            terms.append(gz > 0 if dz < 0 else gz < NGZ - 1)
        return terms[0] if len(terms) == 1 else jnp.logical_and(terms[0], terms[1])

    def ring_device(offset, flip=False):
        q = lax.rem(along + (offset % ring), ring)
        c = 1 - core if flip else core
        return {"gx": lax.div(q, NGZ) * 2 + c, "gy": gy, "gz": lax.rem(q, NGZ)}

    def row_device(offset, flip=False):
        c = 1 - core if flip else core
        return {"gx": gx - core + c, "gy": lax.rem(gy + offset, NGY), "gz": gz}

    def plane_device(dy, dx, flip=False):
        y, x = lax.rem(lax.div(gy, 4) + dy, 4), lax.rem(lax.rem(gy, 4) + dx, 4)
        c = 1 - core if flip else core
        return {"gx": gx - core + c, "gy": y * 4 + x, "gz": gz}

    def block_device(dx, dy, dz):
        return {"gx": gx + dx, "gy": gy + dy, "gz": gz + dz}

    sides = [(dy, dz) for dy in (-1, 0, 1) for dz in (-1, 0, 1) if (dy, dz) != (0, 0)]
    side_buffer = {
        (0, -1): ZL, (0, 1): ZU, (-1, 0): YL, (1, 0): YU,
        (-1, -1): CLL, (-1, 1): CLU, (1, -1): CUL, (1, 1): CUU,
    }

    for (dy, dz), buffer in side_buffer.items():
        @pl.when(jnp.logical_not(both(dy, dz)))
        def _(buffer=buffer):
            buffer[...] = jnp.zeros_like(buffer)
    SR[...] = jnp.zeros_like(SR)

    barrier = pltpu.get_barrier_semaphore()

    def tell(device, semaphore):
        pl.semaphore_signal(semaphore, inc=1, device_id=device, device_id_type=MESH)

    near = [ring_device(o) for o in sorted({1, 2, ring - 1, ring - 2})]
    if NGY == 16:
        plane = [plane_device(*o) for o in ((0, 1), (0, 3), (1, 0), (3, 0))]
        plane_far = [plane_device(*o) for o in ((0, 2), (2, 0))]
    else:
        plane, plane_far = [row_device(o) for o in range(1, NGY)], []
    flipped = row_device(0, True)
    relays = [
        ([ring_device(o) for o in (2, -2)] if ring >= 8 else []) + plane,
        ([ring_device(o) for o in (4, -4)] if ring >= 16 else []) + plane_far,
        [flipped],
        [ring_device(o) for o in (8, -8)] if ring >= 32 else [],
    ]

    def relay_tell(step):
        for device in relays[step]:
            tell(device, relay.at[step])

    def relay_wait(step):
        if relays[step]:
            pl.semaphore_wait(relay.at[step], len(relays[step]))

    @pl.when(jnp.logical_and(gx < pivot - 1, core == 1))
    def _():
        tell(block_device(1, 0, 0), barrier)

    awaited = jnp.logical_and(gives_left, core == 0).astype(jnp.int32)
    for dy, dz in sorted(sides, key=lambda side: -abs(side[0]) - abs(side[1])):
        @pl.when(both(dy, dz))
        def _(dy=dy, dz=dz):
            tell(block_device(0, dy, dz), barrier)
        awaited = awaited + both(dy, dz).astype(jnp.int32)
    for device in near + plane + [flipped]:
        tell(device, barrier)
        awaited = awaited + 1

    loads = [
        pltpu.make_async_copy(classes_hbm, classes_v, in_sem.at[0]),
        pltpu.make_async_copy(densities_hbm, table_v, in_sem.at[1]),
        pltpu.make_async_copy(load_hbm, load_v, in_sem.at[2]),
    ]
    for copy in loads:
        copy.start()

    lane = lax.broadcasted_iota(jnp.int32, (8, 128), 1)
    sub = lax.broadcasted_iota(jnp.int32, (8, 128), 0)
    lane1 = lax.broadcasted_iota(jnp.int32, (1, 128), 1)
    third, third1 = lax.div(lane, 3), lax.div(lane1, 3)

    cells_v[...] = jnp.zeros_like(cells_v)
    loads[0].wait()
    cells_v[:, 0:7, 0:127] = classes_v[...]
    loads[1].wait()
    rho = table_v[...]
    rho = jnp.concatenate([rho, rho], axis=1)
    table = wide(soft_floor + rho * rho * rho * (1.0 - soft_floor))
    inside = jnp.logical_and(sub < 7, lane < 127)
    previous = jnp.zeros((8, 128), jnp.float32)
    for z in range(8):
        if z < 7:
            picked = jnp.take_along_axis(table, cells_v[z], axis=1, mode="promise_in_bounds")
            s = jnp.where(inside, picked, 0.0)
        else:
            s = jnp.zeros((8, 128), jnp.float32)
        S[z, 4] = s
        s = s + roll(s, 1, 1)
        s = s + roll(s, 1, 0)
        S[z, 3] = s + previous
        previous = s
    loads[2].wait()
    for z in range(8):
        for c in range(3):
            S[z, c] = load_v[c, z]
    for f in range(4):
        YH[f] = jnp.concatenate([S[z, f, 7:8, :] for z in range(8)], axis=0)
        YLO[f] = jnp.concatenate([S[z, f, 0:1, :] for z in range(8)], axis=0)
        YLO[4 + f] = jnp.concatenate([S[z, f, 1:2, :] for z in range(8)], axis=0)
    YLO[8] = jnp.concatenate([S[z, 4, 0:1, :] for z in range(8)], axis=0)

    pl.semaphore_wait(barrier, awaited)

    def remote(source, target, sends, recvs, index, device):
        return pltpu.make_async_remote_copy(
            src_ref=source, dst_ref=target, send_sem=sends.at[index], recv_sem=recvs.at[index],
            device_id=device, device_id_type=MESH,
        )

    source_of = {
        (0, -1): S.at[pl.ds(0, 2)],
        (0, 1): S.at[7, pl.ds(0, 4)],
        (-1, 0): YLO,
        (1, 0): YH,
        (-1, -1): YLO.at[:, pl.ds(0, 2)],
        (-1, 1): YLO.at[pl.ds(0, 8), pl.ds(7, 1)],
        (1, -1): YH.at[:, pl.ds(0, 2)],
        (1, 1): YH.at[:, pl.ds(7, 1)],
    }
    y_copies = {
        (dy, dz): remote(source_of[dy, dz], side_buffer[-dy, -dz], y_send, y_recv, sides.index((dy, dz)), block_device(0, dy, dz))
        for dy, dz in sides
    }
    for dy, dz in sorted(sides, key=lambda side: -abs(side[0]) - abs(side[1])):
        @pl.when(both(dy, dz))
        def _(copy=y_copies[dy, dz]):
            copy.start()
    relay_tell(0)
    relay_wait(0)
    relay_tell(1)
    for dy, dz in sides:
        @pl.when(both(dy, dz))
        def _(copy=y_copies[-dy, -dz]):
            copy.wait_recv()

    top, bottom = sub == 0, sub == 7
    for f in range(4):
        low = YL[f] + jnp.where(top, wide(CLL[f]), 0.0) + jnp.where(bottom, wide(CLU[f, 0:1]), 0.0)
        low8 = CLU[f, 1:2]
        high = YU[f] + jnp.where(top, wide(CUL[f]), 0.0) + jnp.where(bottom, wide(CUU[f, 0:1]), 0.0)
        high8 = CUU[f, 1:2]
        G[f, 0:8] = YU[4 + f] + jnp.where(top, wide(CUL[4 + f]), 0.0) + jnp.where(bottom, wide(CUU[4 + f, 0:1]), 0.0)
        G[f, 8:9] = CUU[4 + f, 1:2]
        for z in range(9):
            tile = S[z, f] if z < 8 else ZU[1, f]
            if z == 0:
                tile = tile + ZL[f]
            if z == 7:
                tile = tile + ZU[0, f]
            lower = low[z : z + 1] if z < 8 else low8
            upper = high[z : z + 1] if z < 8 else high8
            A[z, f] = tile + jnp.where(top, wide(lower), 0.0) + jnp.where(bottom, wide(upper), 0.0)
    edge = YU[8]
    for z in range(8):
        tile = S[z, 4] if z < 7 else ZU[0, 4]
        row = edge[z : z + 1] if z < 7 else CUU[8, 0:1]
        A[z, 4] = jnp.where(bottom, wide(row), tile)

    low_tile = high_tile = jnp.zeros((8, 128), jnp.float32)
    low_row = high_row = jnp.zeros((1, 128), jnp.float32)
    for f in range(4):
        for z in range(9):
            k = 9 * f + z
            tile = roll(A[z, f], 3 * k - 125, 1)
            high_tile = jnp.where(third == k, tile, high_tile)
            low_tile = jnp.where(third == k + 1, tile, low_tile)
            row = roll(G[f, z : z + 1], 3 * k - 125, 1)
            high_row = jnp.where(third1 == k, row, high_row)
            low_row = jnp.where(third1 == k + 1, row, low_row)
    for z in range(8):
        tile = roll(A[z, 4], 108 + 2 * z - 125, 1)
        high_tile = jnp.where(lax.div(lane - 108, 2) == z if z else jnp.logical_or(lane == 108, lane == 109), tile, high_tile)
        low_tile = jnp.where(lax.div(lane - 111, 2) == z if z else jnp.logical_or(lane == 111, lane == 112), tile, low_tile)
    for buffer, tile, row in ((SL, high_tile, high_row), (SU, low_tile, low_row)):
        buffer[0:8] = tile
        buffer[8:9] = row
        buffer[9:16] = jnp.zeros((7, 128), jnp.float32)

    nine = pl.ds(0, 9)
    to_left = remote(SU.at[nine], SR.at[nine], x_send, x_recv, 0, block_device(-1, 0, 0))
    to_right = remote(SL.at[nine], SR.at[nine], x_send, x_recv, 1, block_device(1, 0, 0))

    @pl.when(gives_left)
    def _():
        to_left.start()

    def relay_far():
        relay_wait(1)
        relay_tell(2)
        relay_wait(2)

    @pl.when(gives_right)
    def _():
        relay_far()
        to_right.start()

    keep = jnp.logical_or(lane > 0, gx > 0)
    keep1 = jnp.logical_or(lane1 > 0, gx > 0)
    inv_side = inverse(G[3, 0:8])
    inv_corner = inverse(G[3, 8:9])

    def along_x(p):
        q = roll(p, -1, 1)
        return p + q, q - p

    side = [along_x(jnp.where(keep, G[c, 0:8], 0.0) * inv_side) for c in range(3)]
    corner = [along_x(jnp.where(keep1, G[c, 8:9], 0.0) * inv_corner) for c in range(3)]
    owned = jnp.logical_and(
        jnp.logical_and(jnp.logical_or(lane > 1, gx == 0), jnp.logical_or(lane < 126, gx == NGX - 1)),
        jnp.logical_or(sub > 0, gy == 0),
    )
    owned_first = jnp.logical_and(owned, gz == 0)
    rz = jnp.zeros((8, 128), jnp.float32)
    for z in range(9):
        inv = inverse(A[z, 3])
        INV[z] = inv
        for c in range(3):
            start = jnp.where(keep, A[z, c], 0.0)
            p = start * inv
            if z < 8:
                A[z, c] = start
                rz = rz + jnp.where(owned if z else owned_first, start * p, 0.0)
            sums = along_x(p)
            for m in range(2):
                XM[z, c, m, 0:8] = sums[m]
                XM[z, c, m, 8:9] = side[c][m][z : z + 1] if z < 8 else corner[c][m]

    def plane_modes(z):
        modes = {}
        for c in range(3):
            for mx in range(2):
                here, above = XM[z, c, mx, 0:8], XM[z, c, mx, 1:9]
                modes[c, mx, 0] = here + above
                modes[c, mx, 1] = above - here
        return modes

    def spread(first, second, axis, mask):
        return first - second + jnp.where(mask, roll(first + second, 1, axis), 0.0)

    curvature = jnp.zeros((8, 128), jnp.float32)
    square = jnp.zeros((8, 128), jnp.float32)
    lower = plane_modes(0)
    carried = None
    for z in range(8):
        upper = plane_modes(z + 1)
        u = {}
        for key in lower:
            u[key + (0,)] = lower[key] + upper[key]
            u[key + (1,)] = upper[key] - lower[key]
        f = apply_modes(u, A[z, 4])
        here, carry = {}, {}
        for c in range(3):
            for mx in range(2):
                for my in range(2):
                    first, second = f[c, mx, my, 0], f[c, mx, my, 1]
                    if first is None:
                        here[c, mx, my], carry[c, mx, my] = -second, second
                    else:
                        here[c, mx, my], carry[c, mx, my] = first - second, first + second
        if carried is not None:
            here = {key: here[key] + carried[key] for key in here}
        carried = carry
        lower = upper
        inv = INV[z]
        mask = owned if z else owned_first
        for c in range(3):
            rows = [spread(here[c, mx, 0], here[c, mx, 1], 0, sub > 0) for mx in range(2)]
            image = jnp.where(keep, spread(rows[0], rows[1], 1, lane > 0), 0.0)
            IM[z, c] = image
            scaled = image * inv
            curvature = curvature + jnp.where(mask, A[z, c] * scaled, 0.0)
            square = square + jnp.where(mask, image * scaled, 0.0)

    @pl.when(jnp.logical_not(gives_right))
    def _():
        relay_far()

    relay_tell(3)

    @pl.when(jnp.logical_and(has_face, jnp.logical_not(mirrored)))
    def _():
        to_left.wait_recv()

    @pl.when(jnp.logical_and(has_face, mirrored))
    def _():
        to_right.wait_recv()

    lane16 = lax.broadcasted_iota(jnp.int32, (16, 128), 1)
    sub16 = lax.broadcasted_iota(jnp.int32, (16, 128), 0)
    place = lax.rem(lane16, 64)
    column, layer = lax.rem(place, 3), lax.div(place, 3)
    counted = jnp.logical_and(
        jnp.logical_and(
            jnp.logical_and(sub16 < 8, jnp.logical_or(sub16 > 0, gy == 0)),
            jnp.logical_and(layer < 8, jnp.logical_or(layer > 0, gz == 0)),
        ),
        jnp.logical_and(has_face, jnp.where(lane16 < 64, column, 2 - 2 * jnp.abs(column - 1)) > 0),
    )
    received = SR[...]
    sums, for_lower, for_upper = strip_sums(
        jnp.where(mirrored, received, SL[...]), jnp.where(mirrored, SU[...], received), counted
    )
    rz, curvature, square = (
        total_of(own + part[0:8] + part[8:16]) for own, part in zip((rz, curvature, square), sums)
    )

    row = jnp.where(lane1 == 0, rz, jnp.where(lane1 == 1, curvature, square))
    rows_v[0:1] = row
    RA[0:1] = row
    def hops(k):
        return min(k % 4, 4 - k % 4) + min(k // 4, 4 - k // 4)

    for k in sorted(range(NGY), key=lambda k: -hops(k)):
        for flip in (True, False):
            if k or flip:
                device = plane_device(k // 4, k % 4, flip) if NGY == 16 else row_device(k, flip)
                slot = k + (NGY if flip else 0)
                remote(rows_v.at[pl.ds(0, 1)], RA.at[pl.ds(slot, 1)], a_send, a_recv, 0, device).start()

    RS[0] = for_lower
    RS[1] = for_upper
    result_right = remote(RS.at[1], LOW, f_send, f_recv, 3, block_device(1, 0, 0))
    result_left = remote(RS.at[0], HIGH, f_send, f_recv, 4, block_device(-1, 0, 0))
    normal_face = jnp.logical_and(has_face, jnp.logical_not(mirrored))
    mirrored_face = jnp.logical_and(has_face, mirrored)

    @pl.when(normal_face)
    def _():
        result_right.start()
        HIGH[...] = for_lower

    @pl.when(mirrored_face)
    def _():
        result_left.start()
        LOW[...] = for_upper

    def drain(ref, count, semaphore):
        block = ref.at[pl.ds(0, count)]
        pltpu.make_async_copy(block, block, semaphore).wait()

    drain(RA, 2 * NGY - 1, a_recv.at[0])
    row = jnp.sum(RA[...], axis=0, keepdims=True)
    rows_v[1:2] = row
    RB[0:1] = row
    relay_wait(3)
    for k in sorted(range(1, ring), key=lambda k: -min(k, ring - k)):
        remote(rows_v.at[pl.ds(1, 1)], RB.at[pl.ds(k, 1)], a_send, a_recv, 1, ring_device(k)).start()

    @pl.when(gives_left)
    def _():
        result_right.wait_recv()

    @pl.when(jnp.logical_or(gives_left, mirrored_face))
    def _():
        tile = LOW[...]
        for z in range(8):
            diagonal = roll(tile, -(72 + 3 * z), 1)
            INV[z] = jnp.where(lane == 0, inverse(diagonal), INV[z])
            for c in range(3):
                k = 24 * c + 3 * z
                IM[z, c] = jnp.where(lane < 2, roll(tile, -k, 1), IM[z, c])
                A[z, c] = jnp.where(lane == 0, roll(tile, -(k + 2), 1), A[z, c])

    @pl.when(gives_right)
    def _():
        result_left.wait_recv()

    @pl.when(jnp.logical_or(gives_right, normal_face))
    def _():
        tile = HIGH[...]
        for z in range(8):
            diagonal = roll(tile, 127 - (72 + 3 * z + 2), 1)
            INV[z] = jnp.where(lane == 127, inverse(diagonal), INV[z])
            for c in range(3):
                k = 24 * c + 3 * z
                IM[z, c] = jnp.where(lane > 125, roll(tile, 127 - (k + 2), 1), IM[z, c])
                A[z, c] = jnp.where(lane == 127, roll(tile, 127 - k, 1), A[z, c])

    for c in range(3):
        FYS[c] = jnp.concatenate([IM[z, c, 7:8, :] for z in range(8)], axis=0)
    z_fix = remote(IM.at[7], FZ, f_send, f_recv, 0, block_device(0, 0, 1))
    y_fix = remote(FYS, FY, f_send, f_recv, 1, block_device(0, 1, 0))
    yz_fix = remote(FYS.at[:, pl.ds(7, 1)], FYZ, f_send, f_recv, 2, block_device(0, 1, 1))
    fixes = ((yz_fix, 1, 1), (y_fix, 1, 0), (z_fix, 0, 1))
    for copy, dy, dz in fixes:
        @pl.when(both(dy, dz))
        def _(copy=copy):
            copy.start()
    for dy, dz in sides:
        @pl.when(both(dy, dz))
        def _(copy=y_copies[dy, dz]):
            copy.wait_send()
    for copy, dy, dz in fixes:
        @pl.when(both(-dy, -dz))
        def _(copy=copy):
            copy.wait_recv()
    for copy, dy, dz in fixes:
        @pl.when(both(dy, dz))
        def _(copy=copy):
            copy.wait_send()

    @pl.when(gz > 0)
    def _():
        IM[0] = FZ[...]

    @pl.when(gy > 0)
    def _():
        for c in range(3):
            for z in range(8):
                IM[z, c, 0:1, :] = FY[c, z : z + 1, :]

    @pl.when(both(-1, -1))
    def _():
        for c in range(3):
            IM[0, c, 0:1, :] = FYZ[c]

    for copy, condition in (
        (to_left, gives_left), (to_right, gives_right), (result_right, normal_face), (result_left, mirrored_face),
    ):
        @pl.when(condition)
        def _(copy=copy):
            copy.wait_send()
    drain(RA, 2 * NGY - 1, a_send.at[0])
    drain(RB, ring - 1, a_recv.at[1])
    row = jnp.sum(RB[...], axis=0, keepdims=True)
    rz, curvature, square = (row[:, i : i + 1] for i in range(3))
    alpha = rz / curvature
    beta = alpha * alpha * square / rz - 1.0
    alpha, beta = wide(alpha), wide(beta)
    for z in range(8):
        inv = INV[z]
        for c in range(3):
            start = A[z, c]
            p = start * inv
            residual = start - alpha * IM[z, c]
            displacement_ref[c, z] = alpha * p
            residual_ref[c, z] = residual
            direction_ref[c, z] = residual * inv + beta * p
    drain(RB, ring - 1, a_send.at[1])


def store_kernel(a_ref, b_ref, c_ref, a_out, b_out, c_out, sem):
    copies = [
        pltpu.make_async_copy(source, target, sem.at[i])
        for i, (source, target) in enumerate(((a_ref, a_out), (b_ref, b_out), (c_ref, c_out)))
    ]
    for copy in copies:
        copy.start()
    for copy in copies:
        copy.wait()


def on_device(shape, load, classes, densities):
    f32, i32 = jnp.float32, jnp.int32
    ring = shape[0] // 2 * shape[2]
    dma = pltpu.SemaphoreType.DMA

    def rows(n):
        return pltpu.VMEM((n, 128), f32)

    def tiles(*dims):
        return pltpu.VMEM(dims + (8, 128), f32)

    out = jax.ShapeDtypeStruct(load.shape, f32)
    outs = pl.pallas_call(
        functools.partial(kernel, shape),
        out_shape=(out, out, out),
        in_specs=[pl.BlockSpec(memory_space=pltpu.HBM)] * 3,
        out_specs=(pl.BlockSpec(memory_space=pltpu.VMEM),) * 3,
        scratch_shapes=[
            pltpu.VMEM(load.shape, f32), pltpu.VMEM(classes.shape, i32), pltpu.VMEM((1, 64), f32), pltpu.VMEM((7, 8, 128), i32),
            tiles(8, 5), tiles(4), tiles(2, 5), tiles(4), tiles(9), tiles(4), tiles(9),
            pltpu.VMEM((4, 1, 128), f32), pltpu.VMEM((4, 2, 128), f32), pltpu.VMEM((8, 1, 128), f32), pltpu.VMEM((9, 2, 128), f32),
            tiles(9, 5), pltpu.VMEM((4, 16, 128), f32), rows(16), rows(16), rows(16),
            pltpu.VMEM((9, 3, 2, 16, 128), f32), tiles(8, 3), tiles(9),
            tiles(3), tiles(3), tiles(3), pltpu.VMEM((3, 1, 128), f32), tiles(2), tiles(), tiles(),
            rows(2 * shape[1]), rows(ring), rows(2),
            dma((3,)), dma((8,)), dma((8,)), dma((2,)), dma((2,)), dma((5,)), dma((5,)), dma((2,)), dma((2,)),
            pltpu.SemaphoreType.REGULAR((4,)),
        ],
        compiler_params=pltpu.CompilerParams(collective_id=0, has_side_effects=True, vmem_limit_bytes=8 * 2**20),
        name="step",
    )(*(pltpu.with_memory_space_constraint(x, pltpu.HBM) for x in (load, classes, densities.reshape(1, 64))))
    return pl.pallas_call(
        store_kernel,
        out_shape=(out, out, out),
        in_specs=[pl.BlockSpec(memory_space=pltpu.VMEM)] * 3,
        out_specs=(pl.BlockSpec(memory_space=pl.ANY),) * 3,
        scratch_shapes=[dma((3,))],
        compiler_params=pltpu.CompilerParams(vmem_limit_bytes=2 * 2**20),
        name="store",
    )(*outs)


def solution(mesh):
    shape = tuple(mesh.shape[a] for a in ("gx", "gy", "gz"))
    spec = P(None, "gz", "gy", "gx")
    return jax.shard_map(
        functools.partial(on_device, shape), mesh=mesh,
        in_specs=(spec, P("gz", "gy", "gx"), P()), out_specs=(spec, spec, spec), check_vma=False,
    )
```

```python
import functools
import math

import jax
import jax.numpy as jnp
import numpy as np
from jax import lax
from jax.experimental import pallas as pl
from jax.experimental.pallas import tpu as pltpu
from jax.sharding import PartitionSpec as P

MESH = pl.DeviceIdType.MESH
soft_floor = 0.001
poisson = 0.3
lame = poisson / ((1.0 + poisson) * (1.0 - 2.0 * poisson))
shear = 0.5 / (1.0 + poisson)

MASS = (0.25, 1.0 / 12.0)
MODES = [(mx, my, mz) for mx in (0, 1) for my in (0, 1) for mz in (0, 1)]


def mode_couplings():
    rows = {(c, m): [] for c in range(3) for m in MODES}
    for c in range(3):
        for m in MODES:
            own = 0.0
            for axis in range(3):
                if m[axis] == 1:
                    factor = lame + 2.0 * shear if axis == c else shear
                    others = [MASS[m[o]] for o in range(3) if o != axis]
                    own += factor * others[0] * others[1]
            if own:
                rows[c, m].append((own, c, m))
            for k in range(3):
                if k == c:
                    continue
                rest = 3 - c - k
                if m[c] == 1 and m[k] == 0:
                    factor = lame
                elif m[c] == 0 and m[k] == 1:
                    factor = shear
                else:
                    continue
                partner = list(m)
                partner[c], partner[k] = m[k], m[c]
                rows[c, m].append((factor * 0.25 * MASS[m[rest]], k, tuple(partner)))
    return rows


COUPLINGS = mode_couplings()
CORNER_DIAGONAL = sum(w for m in MODES for w, c, _ in COUPLINGS[0, m] if c == 0)


def apply_modes(u, s):
    out = {}
    for c in range(3):
        for m in MODES:
            total = None
            for weight, k, partner in COUPLINGS[c, m]:
                term = u[(k,) + partner] * weight
                total = term if total is None else total + term
            out[(c,) + m] = None if total is None else total * s
    return out


def roll(v, shift, axis):
    return pltpu.roll(v, shift % v.shape[axis], axis)


def inverse(d):
    return 1.0 / jnp.where(d > 0.0, d * CORNER_DIAGONAL, 1.0)


def wide(tile):
    return jnp.broadcast_to(tile, (8, 128))


def total_of(tile):
    return jnp.sum(jnp.sum(tile, axis=0, keepdims=True), axis=1, keepdims=True)


def div(a, n):
    return a >> (n.bit_length() - 1) if n & (n - 1) == 0 else lax.div(a, n)


def rem(a, n):
    return a & (n - 1) if n & (n - 1) == 0 else lax.rem(a, n)


def strip_sums(lower, upper, counted):
    lane = lax.broadcasted_iota(jnp.int32, (16, 128), 1)
    first = lane < 64
    place = lax.rem(lane, 64)
    column, layer = lax.rem(place, 3), lax.div(place, 3)

    def shared(v):
        joined = v + jnp.where(first, roll(v, -62, 1), roll(v, 62, 1))
        return jnp.where(column == jnp.where(first, 2, 0), joined, v)

    def field(f):
        return jnp.where(first, roll(lower, -27 * f, 1), roll(upper, 61 - 27 * f, 1))

    s = jnp.zeros((16, 128), jnp.float32)
    row = lax.broadcasted_iota(jnp.int32, (16, 128), 0)
    for z in range(8):
        found = jnp.where(first, roll(lower, z - 108, 1), roll(upper, z - 111 + 64, 1))
        s = jnp.where(jnp.logical_and(layer == z, column < 2), found, s)
    s = jnp.where(row < 8, s, 0.0)
    d = shared(field(3))
    inv = inverse(d)
    starts, vectors, u = [], [], {}
    for c in range(3):
        start = shared(field(c))
        p = start * inv
        starts.append(start)
        vectors.append(p)
        q = roll(p, -1, 1)
        for mx, along_x in enumerate((p + q, q - p)):
            q = roll(along_x, -1, 0)
            for my, along_y in enumerate((along_x + q, q - along_x)):
                q = roll(along_y, -3, 1)
                u[c, mx, my, 0] = along_y + q
                u[c, mx, my, 1] = q - along_y
    f = apply_modes(u, s)
    rz = curvature = square = jnp.zeros((16, 128), jnp.float32)
    parts = []

    def back(a, b, shift, axis):
        low, high = (-b, b) if a is None else (a - b, a + b)
        return low + roll(high, shift, axis)

    for c in range(3):
        x_parts = []
        for mx in range(2):
            y_parts = [back(f[c, mx, my, 0], f[c, mx, my, 1], 3, 1) for my in range(2)]
            x_parts.append(back(y_parts[0], y_parts[1], 1, 0))
        image = shared(back(x_parts[0], x_parts[1], 1, 1))
        scaled = image * inv
        rz = rz + jnp.where(counted, starts[c] * vectors[c], 0.0)
        curvature = curvature + jnp.where(counted, vectors[c] * image, 0.0)
        square = square + jnp.where(counted, image * scaled, 0.0)
        moved = jnp.where(first, roll(starts[c], -2, 1), roll(starts[c], 2, 1))
        parts.append(jnp.where(column == jnp.where(first, 0, 2), moved, image)[0:8])
    parts.append(d[0:8])
    lane8 = lane[0:8]
    for_lower = for_upper = jnp.zeros((8, 128), jnp.float32)
    for i, part in enumerate(parts):
        here = lax.div(lane8, 24) == i
        for_lower = jnp.where(here, roll(part, 24 * i, 1), for_lower)
        for_upper = jnp.where(here, roll(part, 24 * i - 64, 1), for_upper)
    return (rz, curvature, square), for_lower, for_upper


def kernel(
    shape,
    load_hbm, classes_hbm, densities_hbm,
    displacement_ref, residual_ref, direction_ref,
    load_v, classes_v, table_v, cells_v,
    S, ZL, ZU, YH, YLO, YL, YU, CLL, CLU, CUL, CUU,
    A, G, SL, SU, SR, XM, IM, INV, FZ, FYS, FY, FYZ, RS, LOW, HIGH,
    RA, RB, rows_v,
    in_sem, y_send, y_recv, x_send, x_recv, f_send, f_recv, a_send, a_recv, relay,
):
    NGX, NGY, NGZ = shape
    ring = NGX // 2 * NGZ
    gx, gy, gz = (lax.axis_index(a) for a in ("gx", "gy", "gz"))
    core = rem(gx, 2)
    along = div(gx, 2) * NGZ + gz
    pivot = jnp.where(gz < 5 * NGZ // 8, NGX - 2, NGX - 4)
    mirrored = gx >= pivot
    has_face = jnp.logical_or(jnp.logical_and(mirrored, gx > 0), gx < pivot - 1)
    gives_left = jnp.logical_and(gx >= 1, gx <= pivot - 1)
    gives_right = jnp.logical_and(gx >= pivot - 1, gx <= NGX - 2)

    def both(dy, dz):
        terms = []
        if dy:
            terms.append(gy > 0 if dy < 0 else gy < NGY - 1)
        if dz:
            terms.append(gz > 0 if dz < 0 else gz < NGZ - 1)
        return terms[0] if len(terms) == 1 else jnp.logical_and(terms[0], terms[1])

    def ring_device(offset, flip=False):
        q = rem(along + (offset % ring), ring)
        c = 1 - core if flip else core
        return {"gx": div(q, NGZ) * 2 + c, "gy": gy, "gz": rem(q, NGZ)}

    def row_device(offset, flip=False):
        c = 1 - core if flip else core
        return {"gx": gx - core + c, "gy": rem(gy + offset, NGY), "gz": gz}

    def plane_device(dy, dx, flip=False):
        y, x = rem(div(gy, 4) + dy, 4), rem(rem(gy, 4) + dx, 4)
        c = 1 - core if flip else core
        return {"gx": gx - core + c, "gy": y * 4 + x, "gz": gz}

    def block_device(dx, dy, dz):
        return {"gx": gx + dx, "gy": gy + dy, "gz": gz + dz}

    sides = [(dy, dz) for dy in (-1, 0, 1) for dz in (-1, 0, 1) if (dy, dz) != (0, 0)]
    side_buffer = {
        (0, -1): ZL, (0, 1): ZU, (-1, 0): YL, (1, 0): YU,
        (-1, -1): CLL, (-1, 1): CLU, (1, -1): CUL, (1, 1): CUU,
    }

    for (dy, dz), buffer in side_buffer.items():
        @pl.when(jnp.logical_not(both(dy, dz)))
        def _(buffer=buffer):
            buffer[...] = jnp.zeros_like(buffer)
    SR[...] = jnp.zeros_like(SR)

    barrier = pltpu.get_barrier_semaphore()

    def tell(device, semaphore):
        pl.semaphore_signal(semaphore, inc=1, device_id=device, device_id_type=MESH)

    near = [ring_device(o, flip) for o in sorted({1, 2, ring - 1, ring - 2}) for flip in (False, True)]
    if NGY == 16:
        plane = [plane_device(*o) for o in ((0, 1), (0, 3), (1, 0), (3, 0))]
        plane_far = [plane_device(*o) for o in ((0, 2), (2, 0))]
    else:
        plane, plane_far = [row_device(o) for o in range(1, NGY)], []
    flipped = row_device(0, True)
    relays = [
        ([ring_device(o, flip) for o in (2, -2) for flip in (False, True)] if ring >= 8 else []) + plane,
        ([ring_device(o, flip) for o in (4, -4) for flip in (False, True)] if ring >= 16 else []) + plane_far,
        [flipped],
        [ring_device(o) for o in (8, -8)] if ring >= 32 else [],
    ]

    def relay_tell(step):
        for device in relays[step]:
            tell(device, relay.at[step])

    def relay_wait(step):
        if relays[step]:
            pl.semaphore_wait(relay.at[step], len(relays[step]))

    @pl.when(jnp.logical_and(gx < pivot - 1, core == 1))
    def _():
        tell(block_device(1, 0, 0), barrier)

    awaited = jnp.logical_and(gives_left, core == 0).astype(jnp.int32)
    for dy, dz in sorted(sides, key=lambda side: -abs(side[0]) - abs(side[1])):
        @pl.when(both(dy, dz))
        def _(dy=dy, dz=dz):
            tell(block_device(0, dy, dz), barrier)
        awaited = awaited + both(dy, dz).astype(jnp.int32)
    for device in near + plane + [flipped]:
        tell(device, barrier)
        awaited = awaited + 1

    loads = [
        pltpu.make_async_copy(classes_hbm, classes_v, in_sem.at[0]),
        pltpu.make_async_copy(densities_hbm, table_v, in_sem.at[1]),
        pltpu.make_async_copy(load_hbm, load_v, in_sem.at[2]),
    ]
    for copy in loads:
        copy.start()

    lane = lax.broadcasted_iota(jnp.int32, (8, 128), 1)
    sub = lax.broadcasted_iota(jnp.int32, (8, 128), 0)
    lane1 = lax.broadcasted_iota(jnp.int32, (1, 128), 1)
    third, third1 = lax.div(lane, 3), lax.div(lane1, 3)

    cells_v[...] = jnp.zeros_like(cells_v)
    loads[0].wait()
    cells_v[:, 0:7, 0:127] = classes_v[...]
    loads[1].wait()
    rho = table_v[...]
    rho = jnp.concatenate([rho, rho], axis=1)
    table = wide(soft_floor + rho * rho * rho * (1.0 - soft_floor))
    inside = jnp.logical_and(sub < 7, lane < 127)
    previous = jnp.zeros((8, 128), jnp.float32)
    for z in range(8):
        if z < 7:
            picked = jnp.take_along_axis(table, cells_v[z], axis=1, mode="promise_in_bounds")
            s = jnp.where(inside, picked, 0.0)
        else:
            s = jnp.zeros((8, 128), jnp.float32)
        S[z, 4] = s
        s = s + roll(s, 1, 1)
        s = s + roll(s, 1, 0)
        S[z, 3] = s + previous
        previous = s
    loads[2].wait()
    for z in range(8):
        for c in range(3):
            S[z, c] = load_v[c, z]
    for f in range(4):
        YH[f] = jnp.concatenate([S[z, f, 7:8, :] for z in range(8)], axis=0)
        YLO[f] = jnp.concatenate([S[z, f, 0:1, :] for z in range(8)], axis=0)
        YLO[4 + f] = jnp.concatenate([S[z, f, 1:2, :] for z in range(8)], axis=0)
    YLO[8] = jnp.concatenate([S[z, 4, 0:1, :] for z in range(8)], axis=0)

    pl.semaphore_wait(barrier, awaited)

    def remote(source, target, sends, recvs, index, device):
        return pltpu.make_async_remote_copy(
            src_ref=source, dst_ref=target, send_sem=sends.at[index], recv_sem=recvs.at[index],
            device_id=device, device_id_type=MESH,
        )

    source_of = {
        (0, -1): S.at[pl.ds(0, 2)],
        (0, 1): S.at[7, pl.ds(0, 4)],
        (-1, 0): YLO,
        (1, 0): YH,
        (-1, -1): YLO.at[:, pl.ds(0, 2)],
        (-1, 1): YLO.at[pl.ds(0, 8), pl.ds(7, 1)],
        (1, -1): YH.at[:, pl.ds(0, 2)],
        (1, 1): YH.at[:, pl.ds(7, 1)],
    }
    y_copies = {
        (dy, dz): remote(source_of[dy, dz], side_buffer[-dy, -dz], y_send, y_recv, sides.index((dy, dz)), block_device(0, dy, dz))
        for dy, dz in sides
    }
    for dy, dz in sorted(sides, key=lambda side: -abs(side[0]) - abs(side[1])):
        @pl.when(both(dy, dz))
        def _(copy=y_copies[dy, dz]):
            copy.start()
    relay_tell(0)
    relay_wait(0)
    relay_tell(1)
    for dy, dz in sides:
        @pl.when(both(dy, dz))
        def _(copy=y_copies[-dy, -dz]):
            copy.wait_recv()

    top, bottom = sub == 0, sub == 7
    for f in range(4):
        low = YL[f] + jnp.where(top, wide(CLL[f]), 0.0) + jnp.where(bottom, wide(CLU[f, 0:1]), 0.0)
        low8 = CLU[f, 1:2]
        high = YU[f] + jnp.where(top, wide(CUL[f]), 0.0) + jnp.where(bottom, wide(CUU[f, 0:1]), 0.0)
        high8 = CUU[f, 1:2]
        G[f, 0:8] = YU[4 + f] + jnp.where(top, wide(CUL[4 + f]), 0.0) + jnp.where(bottom, wide(CUU[4 + f, 0:1]), 0.0)
        G[f, 8:9] = CUU[4 + f, 1:2]
        for z in range(9):
            tile = S[z, f] if z < 8 else ZU[1, f]
            if z == 0:
                tile = tile + ZL[f]
            if z == 7:
                tile = tile + ZU[0, f]
            lower = low[z : z + 1] if z < 8 else low8
            upper = high[z : z + 1] if z < 8 else high8
            A[z, f] = tile + jnp.where(top, wide(lower), 0.0) + jnp.where(bottom, wide(upper), 0.0)
    edge = YU[8]
    for z in range(8):
        tile = S[z, 4] if z < 7 else ZU[0, 4]
        row = edge[z : z + 1] if z < 7 else CUU[8, 0:1]
        A[z, 4] = jnp.where(bottom, wide(row), tile)

    low_tile = high_tile = jnp.zeros((8, 128), jnp.float32)
    low_row = high_row = jnp.zeros((1, 128), jnp.float32)
    for f in range(4):
        for z in range(9):
            k = 9 * f + z
            tile = roll(A[z, f], 3 * k - 125, 1)
            high_tile = jnp.where(third == k, tile, high_tile)
            low_tile = jnp.where(third == k + 1, tile, low_tile)
            row = roll(G[f, z : z + 1], 3 * k - 125, 1)
            high_row = jnp.where(third1 == k, row, high_row)
            low_row = jnp.where(third1 == k + 1, row, low_row)
    for z in range(8):
        tile = roll(A[z, 4], 108 + 2 * z - 125, 1)
        high_tile = jnp.where(lax.div(lane - 108, 2) == z if z else jnp.logical_or(lane == 108, lane == 109), tile, high_tile)
        low_tile = jnp.where(lax.div(lane - 111, 2) == z if z else jnp.logical_or(lane == 111, lane == 112), tile, low_tile)
    for buffer, tile, row in ((SL, high_tile, high_row), (SU, low_tile, low_row)):
        buffer[0:8] = tile
        buffer[8:9] = row
        buffer[9:16] = jnp.zeros((7, 128), jnp.float32)

    nine = pl.ds(0, 9)
    to_left = remote(SU.at[nine], SR.at[nine], x_send, x_recv, 0, block_device(-1, 0, 0))
    to_right = remote(SL.at[nine], SR.at[nine], x_send, x_recv, 1, block_device(1, 0, 0))

    @pl.when(gives_left)
    def _():
        to_left.start()

    @pl.when(gives_right)
    def _():
        relay_wait(1)
        to_right.start()

    keep = jnp.logical_or(lane > 0, gx > 0)
    keep1 = jnp.logical_or(lane1 > 0, gx > 0)
    inv_side = inverse(G[3, 0:8])
    inv_corner = inverse(G[3, 8:9])

    def along_x(p):
        q = roll(p, -1, 1)
        return p + q, q - p

    side = [along_x(jnp.where(keep, G[c, 0:8], 0.0) * inv_side) for c in range(3)]
    corner = [along_x(jnp.where(keep1, G[c, 8:9], 0.0) * inv_corner) for c in range(3)]
    owned = jnp.logical_and(
        jnp.logical_and(jnp.logical_or(lane > 1, gx == 0), jnp.logical_or(lane < 126, gx == NGX - 1)),
        jnp.logical_or(sub > 0, gy == 0),
    )
    owned_first = jnp.logical_and(owned, gz == 0)
    rz = jnp.zeros((8, 128), jnp.float32)
    for z in range(9):
        inv = inverse(A[z, 3])
        INV[z] = inv
        for c in range(3):
            start = jnp.where(keep, A[z, c], 0.0)
            p = start * inv
            if z < 8:
                A[z, c] = start
                rz = rz + jnp.where(owned if z else owned_first, start * p, 0.0)
            sums = along_x(p)
            for m in range(2):
                XM[z, c, m, 0:8] = sums[m]
                XM[z, c, m, 8:9] = side[c][m][z : z + 1] if z < 8 else corner[c][m]

    def plane_modes(z):
        modes = {}
        for c in range(3):
            for mx in range(2):
                here, above = XM[z, c, mx, 0:8], XM[z, c, mx, 1:9]
                modes[c, mx, 0] = here + above
                modes[c, mx, 1] = above - here
        return modes

    def spread(first, second, axis, mask):
        return first - second + jnp.where(mask, roll(first + second, 1, axis), 0.0)

    curvature = jnp.zeros((8, 128), jnp.float32)
    square = jnp.zeros((8, 128), jnp.float32)
    lower = plane_modes(0)
    carried = None
    for z in range(8):
        upper = plane_modes(z + 1)
        u = {}
        for key in lower:
            u[key + (0,)] = lower[key] + upper[key]
            u[key + (1,)] = upper[key] - lower[key]
        f = apply_modes(u, A[z, 4])
        here, carry = {}, {}
        for c in range(3):
            for mx in range(2):
                for my in range(2):
                    first, second = f[c, mx, my, 0], f[c, mx, my, 1]
                    if first is None:
                        here[c, mx, my], carry[c, mx, my] = -second, second
                    else:
                        here[c, mx, my], carry[c, mx, my] = first - second, first + second
        if carried is not None:
            here = {key: here[key] + carried[key] for key in here}
        carried = carry
        lower = upper
        inv = INV[z]
        mask = owned if z else owned_first
        for c in range(3):
            rows = [spread(here[c, mx, 0], here[c, mx, 1], 0, sub > 0) for mx in range(2)]
            image = jnp.where(keep, spread(rows[0], rows[1], 1, lane > 0), 0.0)
            IM[z, c] = image
            scaled = image * inv
            curvature = curvature + jnp.where(mask, A[z, c] * scaled, 0.0)
            square = square + jnp.where(mask, image * scaled, 0.0)

    @pl.when(jnp.logical_not(gives_right))
    def _():
        relay_wait(1)

    relay_tell(2)
    relay_wait(2)
    relay_tell(3)

    @pl.when(jnp.logical_and(has_face, jnp.logical_not(mirrored)))
    def _():
        to_left.wait_recv()

    @pl.when(jnp.logical_and(has_face, mirrored))
    def _():
        to_right.wait_recv()

    lane16 = lax.broadcasted_iota(jnp.int32, (16, 128), 1)
    sub16 = lax.broadcasted_iota(jnp.int32, (16, 128), 0)
    place = lax.rem(lane16, 64)
    column, layer = lax.rem(place, 3), lax.div(place, 3)
    counted = jnp.logical_and(
        jnp.logical_and(
            jnp.logical_and(sub16 < 8, jnp.logical_or(sub16 > 0, gy == 0)),
            jnp.logical_and(layer < 8, jnp.logical_or(layer > 0, gz == 0)),
        ),
        jnp.logical_and(has_face, jnp.where(lane16 < 64, column, 2 - 2 * jnp.abs(column - 1)) > 0),
    )
    received = SR[...]
    sums, for_lower, for_upper = strip_sums(
        jnp.where(mirrored, received, SL[...]), jnp.where(mirrored, SU[...], received), counted
    )
    rz, curvature, square = (
        total_of(own + part[0:8] + part[8:16]) for own, part in zip((rz, curvature, square), sums)
    )

    row = jnp.where(lane1 == 0, rz, jnp.where(lane1 == 1, curvature, square))
    rows_v[0:1] = row
    RA[0:1] = row
    def hops(k):
        return min(k % 4, 4 - k % 4) + min(k // 4, 4 - k // 4)

    for k in sorted(range(NGY), key=lambda k: -hops(k)):
        for flip in (True, False):
            if k or flip:
                device = plane_device(k // 4, k % 4, flip) if NGY == 16 else row_device(k, flip)
                slot = k + (NGY if flip else 0)
                remote(rows_v.at[pl.ds(0, 1)], RA.at[pl.ds(slot, 1)], a_send, a_recv, 0, device).start()

    RS[0] = for_lower
    RS[1] = for_upper
    result_right = remote(RS.at[1], LOW, f_send, f_recv, 3, block_device(1, 0, 0))
    result_left = remote(RS.at[0], HIGH, f_send, f_recv, 4, block_device(-1, 0, 0))
    normal_face = jnp.logical_and(has_face, jnp.logical_not(mirrored))
    mirrored_face = jnp.logical_and(has_face, mirrored)

    @pl.when(normal_face)
    def _():
        result_right.start()
        HIGH[...] = for_lower

    @pl.when(mirrored_face)
    def _():
        result_left.start()
        LOW[...] = for_upper

    def drain(ref, count, semaphore):
        block = ref.at[pl.ds(0, count)]
        pltpu.make_async_copy(block, block, semaphore).wait()

    drain(RA, 2 * NGY - 1, a_recv.at[0])
    row = jnp.sum(RA[...], axis=0, keepdims=True)
    rows_v[1:2] = row
    RB[along] = row
    relay_wait(3)
    for k in range(ring - 1):
        chip = jnp.where(k < along, k, k + 1)
        device = {"gx": div(chip, NGZ) * 2 + core, "gy": gy, "gz": rem(chip, NGZ)}
        remote(rows_v.at[pl.ds(1, 1)], RB.at[along], a_send, a_recv, 1, device).start()

    @pl.when(gives_left)
    def _():
        result_right.wait_recv()

    @pl.when(jnp.logical_or(gives_left, mirrored_face))
    def _():
        tile = LOW[...]
        for z in range(8):
            diagonal = roll(tile, -(72 + 3 * z), 1)
            INV[z] = jnp.where(lane == 0, inverse(diagonal), INV[z])
            for c in range(3):
                k = 24 * c + 3 * z
                IM[z, c] = jnp.where(lane < 2, roll(tile, -k, 1), IM[z, c])
                A[z, c] = jnp.where(lane == 0, roll(tile, -(k + 2), 1), A[z, c])

    @pl.when(gives_right)
    def _():
        result_left.wait_recv()

    @pl.when(jnp.logical_or(gives_right, normal_face))
    def _():
        tile = HIGH[...]
        for z in range(8):
            diagonal = roll(tile, 127 - (72 + 3 * z + 2), 1)
            INV[z] = jnp.where(lane == 127, inverse(diagonal), INV[z])
            for c in range(3):
                k = 24 * c + 3 * z
                IM[z, c] = jnp.where(lane > 125, roll(tile, 127 - (k + 2), 1), IM[z, c])
                A[z, c] = jnp.where(lane == 127, roll(tile, 127 - k, 1), A[z, c])

    for c in range(3):
        FYS[c] = jnp.concatenate([IM[z, c, 7:8, :] for z in range(8)], axis=0)
    z_fix = remote(IM.at[7], FZ, f_send, f_recv, 0, block_device(0, 0, 1))
    y_fix = remote(FYS, FY, f_send, f_recv, 1, block_device(0, 1, 0))
    yz_fix = remote(FYS.at[:, pl.ds(7, 1)], FYZ, f_send, f_recv, 2, block_device(0, 1, 1))
    fixes = ((yz_fix, 1, 1), (y_fix, 1, 0), (z_fix, 0, 1))
    for copy, dy, dz in fixes:
        @pl.when(both(dy, dz))
        def _(copy=copy):
            copy.start()
    for dy, dz in sides:
        @pl.when(both(dy, dz))
        def _(copy=y_copies[dy, dz]):
            copy.wait_send()
    for copy, dy, dz in fixes:
        @pl.when(both(-dy, -dz))
        def _(copy=copy):
            copy.wait_recv()
    for copy, dy, dz in fixes:
        @pl.when(both(dy, dz))
        def _(copy=copy):
            copy.wait_send()

    @pl.when(gz > 0)
    def _():
        IM[0] = FZ[...]

    @pl.when(gy > 0)
    def _():
        for c in range(3):
            for z in range(8):
                IM[z, c, 0:1, :] = FY[c, z : z + 1, :]

    @pl.when(both(-1, -1))
    def _():
        for c in range(3):
            IM[0, c, 0:1, :] = FYZ[c]

    for copy, condition in (
        (to_left, gives_left), (to_right, gives_right), (result_right, normal_face), (result_left, mirrored_face),
    ):
        @pl.when(condition)
        def _(copy=copy):
            copy.wait_send()
    drain(RA, 2 * NGY - 1, a_send.at[0])
    drain(RB, ring - 1, a_recv.at[1])
    row = jnp.sum(RB[...], axis=0)
    rz, curvature, square = (row[:, i : i + 1] for i in range(3))
    alpha = rz / curvature
    beta = alpha * alpha * square / rz - 1.0
    alpha, beta = wide(alpha), wide(beta)
    for z in range(8):
        inv = INV[z]
        for c in range(3):
            start = A[z, c]
            p = start * inv
            residual = start - alpha * IM[z, c]
            displacement_ref[c, z] = alpha * p
            residual_ref[c, z] = residual
            direction_ref[c, z] = residual * inv + beta * p
    drain(RB, ring - 1, a_send.at[1])


def store_kernel(a_ref, b_ref, c_ref, a_out, b_out, c_out, sem):
    copies = [
        pltpu.make_async_copy(source, target, sem.at[i])
        for i, (source, target) in enumerate(((a_ref, a_out), (b_ref, b_out), (c_ref, c_out)))
    ]
    for copy in copies:
        copy.start()
    for copy in copies:
        copy.wait()


def on_device(shape, load, classes, densities):
    f32, i32 = jnp.float32, jnp.int32
    ring = shape[0] // 2 * shape[2]
    dma = pltpu.SemaphoreType.DMA

    def rows(n):
        return pltpu.VMEM((n, 128), f32)

    def tiles(*dims):
        return pltpu.VMEM(dims + (8, 128), f32)

    out = jax.ShapeDtypeStruct(load.shape, f32)
    outs = pl.pallas_call(
        functools.partial(kernel, shape),
        out_shape=(out, out, out),
        in_specs=[pl.BlockSpec(memory_space=pltpu.HBM)] * 3,
        out_specs=(pl.BlockSpec(memory_space=pltpu.VMEM),) * 3,
        scratch_shapes=[
            pltpu.VMEM(load.shape, f32), pltpu.VMEM(classes.shape, i32), pltpu.VMEM((1, 64), f32), pltpu.VMEM((7, 8, 128), i32),
            tiles(8, 5), tiles(4), tiles(2, 5), tiles(4), tiles(9), tiles(4), tiles(9),
            pltpu.VMEM((4, 1, 128), f32), pltpu.VMEM((4, 2, 128), f32), pltpu.VMEM((8, 1, 128), f32), pltpu.VMEM((9, 2, 128), f32),
            tiles(9, 5), pltpu.VMEM((4, 16, 128), f32), rows(16), rows(16), rows(16),
            pltpu.VMEM((9, 3, 2, 16, 128), f32), tiles(8, 3), tiles(9),
            tiles(3), tiles(3), tiles(3), pltpu.VMEM((3, 1, 128), f32), tiles(2), tiles(), tiles(),
            rows(2 * shape[1]), pltpu.VMEM((ring, 1, 128), f32), rows(2),
            dma((3,)), dma((8,)), dma((8,)), dma((2,)), dma((2,)), dma((5,)), dma((5,)), dma((2,)), dma((2,)),
            pltpu.SemaphoreType.REGULAR((4,)),
        ],
        compiler_params=pltpu.CompilerParams(collective_id=0, has_side_effects=True, vmem_limit_bytes=8 * 2**20),
        name="step",
    )(*(pltpu.with_memory_space_constraint(x, pltpu.HBM) for x in (load, classes, densities.reshape(1, 64))))
    return pl.pallas_call(
        store_kernel,
        out_shape=(out, out, out),
        in_specs=[pl.BlockSpec(memory_space=pltpu.VMEM)] * 3,
        out_specs=(pl.BlockSpec(memory_space=pl.ANY),) * 3,
        scratch_shapes=[dma((3,))],
        compiler_params=pltpu.CompilerParams(vmem_limit_bytes=2 * 2**20),
        name="store",
    )(*outs)


def solution(mesh):
    shape = tuple(mesh.shape[a] for a in ("gx", "gy", "gz"))
    spec = P(None, "gz", "gy", "gx")
    return jax.shard_map(
        functools.partial(on_device, shape), mesh=mesh,
        in_specs=(spec, P("gz", "gy", "gx"), P()), out_specs=(spec, spec, spec), check_vma=False,
    )
```

```python
import functools
import math

import jax
import jax.numpy as jnp
import numpy as np
from jax import lax
from jax.experimental import pallas as pl
from jax.experimental.pallas import tpu as pltpu
from jax.sharding import PartitionSpec as P

MESH = pl.DeviceIdType.MESH
soft_floor = 0.001
poisson = 0.3
lame = poisson / ((1.0 + poisson) * (1.0 - 2.0 * poisson))
shear = 0.5 / (1.0 + poisson)

MASS = (0.25, 1.0 / 12.0)
MODES = [(mx, my, mz) for mx in (0, 1) for my in (0, 1) for mz in (0, 1)]


def mode_couplings():
    rows = {(c, m): [] for c in range(3) for m in MODES}
    for c in range(3):
        for m in MODES:
            own = 0.0
            for axis in range(3):
                if m[axis] == 1:
                    factor = lame + 2.0 * shear if axis == c else shear
                    others = [MASS[m[o]] for o in range(3) if o != axis]
                    own += factor * others[0] * others[1]
            if own:
                rows[c, m].append((own, c, m))
            for k in range(3):
                if k == c:
                    continue
                rest = 3 - c - k
                if m[c] == 1 and m[k] == 0:
                    factor = lame
                elif m[c] == 0 and m[k] == 1:
                    factor = shear
                else:
                    continue
                partner = list(m)
                partner[c], partner[k] = m[k], m[c]
                rows[c, m].append((factor * 0.25 * MASS[m[rest]], k, tuple(partner)))
    return rows


COUPLINGS = mode_couplings()
CORNER_DIAGONAL = sum(w for m in MODES for w, c, _ in COUPLINGS[0, m] if c == 0)


def apply_modes(u, s):
    out = {}
    for c in range(3):
        for m in MODES:
            total = None
            for weight, k, partner in COUPLINGS[c, m]:
                term = u[(k,) + partner] * weight
                total = term if total is None else total + term
            out[(c,) + m] = None if total is None else total * s
    return out


def roll(v, shift, axis):
    return pltpu.roll(v, shift % v.shape[axis], axis)


def inverse(d):
    return 1.0 / jnp.where(d > 0.0, d * CORNER_DIAGONAL, 1.0)


def wide(tile):
    return jnp.broadcast_to(tile, (8, 128))


def total_of(tile):
    return jnp.sum(jnp.sum(tile, axis=0, keepdims=True), axis=1, keepdims=True)


def div(a, n):
    return a >> (n.bit_length() - 1) if n & (n - 1) == 0 else lax.div(a, n)


def rem(a, n):
    return a & (n - 1) if n & (n - 1) == 0 else lax.rem(a, n)


def strip_sums(lower, upper, counted):
    lane = lax.broadcasted_iota(jnp.int32, (16, 128), 1)
    first = lane < 64
    place = lax.rem(lane, 64)
    column, layer = lax.rem(place, 3), lax.div(place, 3)

    def shared(v):
        joined = v + jnp.where(first, roll(v, -62, 1), roll(v, 62, 1))
        return jnp.where(column == jnp.where(first, 2, 0), joined, v)

    def field(f):
        return jnp.where(first, roll(lower, -27 * f, 1), roll(upper, 61 - 27 * f, 1))

    s = jnp.zeros((16, 128), jnp.float32)
    row = lax.broadcasted_iota(jnp.int32, (16, 128), 0)
    for z in range(8):
        found = jnp.where(first, roll(lower, z - 108, 1), roll(upper, z - 111 + 64, 1))
        s = jnp.where(jnp.logical_and(layer == z, column < 2), found, s)
    s = jnp.where(row < 8, s, 0.0)
    d = shared(field(3))
    inv = inverse(d)
    starts, vectors, u = [], [], {}
    for c in range(3):
        start = shared(field(c))
        p = start * inv
        starts.append(start)
        vectors.append(p)
        q = roll(p, -1, 1)
        for mx, along_x in enumerate((p + q, q - p)):
            q = roll(along_x, -1, 0)
            for my, along_y in enumerate((along_x + q, q - along_x)):
                q = roll(along_y, -3, 1)
                u[c, mx, my, 0] = along_y + q
                u[c, mx, my, 1] = q - along_y
    f = apply_modes(u, s)
    rz = curvature = square = jnp.zeros((16, 128), jnp.float32)
    parts = []

    def back(a, b, shift, axis):
        low, high = (-b, b) if a is None else (a - b, a + b)
        return low + roll(high, shift, axis)

    for c in range(3):
        x_parts = []
        for mx in range(2):
            y_parts = [back(f[c, mx, my, 0], f[c, mx, my, 1], 3, 1) for my in range(2)]
            x_parts.append(back(y_parts[0], y_parts[1], 1, 0))
        image = shared(back(x_parts[0], x_parts[1], 1, 1))
        scaled = image * inv
        rz = rz + jnp.where(counted, starts[c] * vectors[c], 0.0)
        curvature = curvature + jnp.where(counted, vectors[c] * image, 0.0)
        square = square + jnp.where(counted, image * scaled, 0.0)
        moved = jnp.where(first, roll(starts[c], -2, 1), roll(starts[c], 2, 1))
        parts.append(jnp.where(column == jnp.where(first, 0, 2), moved, image)[0:8])
    parts.append(d[0:8])
    lane8 = lane[0:8]
    for_lower = for_upper = jnp.zeros((8, 128), jnp.float32)
    for i, part in enumerate(parts):
        here = lax.div(lane8, 24) == i
        for_lower = jnp.where(here, roll(part, 24 * i, 1), for_lower)
        for_upper = jnp.where(here, roll(part, 24 * i - 64, 1), for_upper)
    return (rz, curvature, square), for_lower, for_upper


def kernel(
    shape,
    load_hbm, classes_hbm, densities_hbm,
    displacement_ref, residual_ref, direction_ref,
    load_v, classes_v, table_v, cells_v,
    S, ZL, ZU, YH, YLO, YL, YU, CLL, CLU, CUL, CUU,
    A, G, SL, SU, SR, XM, IM, INV, FZ, FYS, FY, FYZ, RS, LOW, HIGH,
    RA, RB, rows_v,
    in_sem, y_send, y_recv, x_send, x_recv, f_send, f_recv, a_send, a_recv, relay,
):
    NGX, NGY, NGZ = shape
    ring = NGX // 2 * NGZ
    gx, gy, gz = (lax.axis_index(a) for a in ("gx", "gy", "gz"))
    core = rem(gx, 2)
    along = div(gx, 2) * NGZ + gz
    pivot = jnp.where(gz < 5 * NGZ // 8, NGX - 2, NGX - 4)
    mirrored = gx >= pivot
    has_face = jnp.logical_or(jnp.logical_and(mirrored, gx > 0), gx < pivot - 1)
    gives_left = jnp.logical_and(gx >= 1, gx <= pivot - 1)
    gives_right = jnp.logical_and(gx >= pivot - 1, gx <= NGX - 2)

    def both(dy, dz):
        terms = []
        if dy:
            terms.append(gy > 0 if dy < 0 else gy < NGY - 1)
        if dz:
            terms.append(gz > 0 if dz < 0 else gz < NGZ - 1)
        return terms[0] if len(terms) == 1 else jnp.logical_and(terms[0], terms[1])

    def ring_device(offset, flip=False):
        q = rem(along + (offset % ring), ring)
        c = 1 - core if flip else core
        return {"gx": div(q, NGZ) * 2 + c, "gy": gy, "gz": rem(q, NGZ)}

    def row_device(offset, flip=False):
        c = 1 - core if flip else core
        return {"gx": gx - core + c, "gy": rem(gy + offset, NGY), "gz": gz}

    def plane_device(dy, dx, flip=False):
        y, x = rem(div(gy, 4) + dy, 4), rem(rem(gy, 4) + dx, 4)
        c = 1 - core if flip else core
        return {"gx": gx - core + c, "gy": y * 4 + x, "gz": gz}

    def block_device(dx, dy, dz):
        return {"gx": gx + dx, "gy": gy + dy, "gz": gz + dz}

    sides = [(dy, dz) for dy in (-1, 0, 1) for dz in (-1, 0, 1) if (dy, dz) != (0, 0)]
    side_buffer = {
        (0, -1): ZL, (0, 1): ZU, (-1, 0): YL, (1, 0): YU,
        (-1, -1): CLL, (-1, 1): CLU, (1, -1): CUL, (1, 1): CUU,
    }

    loads = [
        pltpu.make_async_copy(classes_hbm, classes_v, in_sem.at[0]),
        pltpu.make_async_copy(densities_hbm, table_v, in_sem.at[1]),
        pltpu.make_async_copy(load_hbm, load_v, in_sem.at[2]),
    ]
    for copy in loads:
        copy.start()

    for (dy, dz), buffer in side_buffer.items():
        @pl.when(jnp.logical_not(both(dy, dz)))
        def _(buffer=buffer):
            buffer[...] = jnp.zeros_like(buffer)
    SR[...] = jnp.zeros_like(SR)

    barrier = pltpu.get_barrier_semaphore()

    def tell(device, semaphore):
        pl.semaphore_signal(semaphore, inc=1, device_id=device, device_id_type=MESH)

    two_away = [ring_device(o, flip) for o in sorted({2, ring - 2}) for flip in (False, True)]
    one_away = [ring_device(o) for o in (1, -1)] if ring > 2 else []
    if NGY == 16:
        plane = [plane_device(*o) for o in ((0, 1), (0, 3), (1, 0), (3, 0))]
        plane_far = [plane_device(*o) for o in ((0, 2), (2, 0))]
    else:
        plane, plane_far = [row_device(o) for o in range(1, NGY)], []
    flipped = row_device(0, True)
    relays = [
        ([ring_device(o, flip) for o in (2, -2) for flip in (False, True)] if ring >= 8 else []) + plane,
        ([ring_device(o, flip) for o in (4, -4) for flip in (False, True)] if ring >= 16 else []) + plane_far,
        [flipped],
        [ring_device(o) for o in (8, -8)] if ring >= 32 else [],
    ]

    def relay_tell(step):
        for device in relays[step]:
            tell(device, relay.at[step])

    def relay_wait(step):
        if relays[step]:
            pl.semaphore_wait(relay.at[step], len(relays[step]))

    @pl.when(jnp.logical_and(gx < pivot - 1, core == 1))
    def _():
        tell(block_device(1, 0, 0), barrier)

    awaited = jnp.logical_and(gives_left, core == 0).astype(jnp.int32)

    def tell_side(dy, dz):
        @pl.when(both(dy, dz))
        def _():
            tell(block_device(0, dy, dz), barrier)
        return both(dy, dz).astype(jnp.int32)

    for dy, dz in sides:
        if dy and dz:
            awaited = awaited + tell_side(dy, dz)
    for device in two_away:
        tell(device, barrier)
    for dy, dz in sides:
        if not (dy and dz):
            awaited = awaited + tell_side(dy, dz)
    for device in plane + one_away + [flipped]:
        tell(device, barrier)
    awaited = awaited + len(two_away + plane + one_away + [flipped])

    lane = lax.broadcasted_iota(jnp.int32, (8, 128), 1)
    sub = lax.broadcasted_iota(jnp.int32, (8, 128), 0)
    lane1 = lax.broadcasted_iota(jnp.int32, (1, 128), 1)
    third, third1 = lax.div(lane, 3), lax.div(lane1, 3)

    cells_v[...] = jnp.zeros_like(cells_v)
    loads[0].wait()
    cells_v[:, 0:7, 0:127] = classes_v[...]
    loads[1].wait()
    rho = table_v[...]
    rho = jnp.concatenate([rho, rho], axis=1)
    table = wide(soft_floor + rho * rho * rho * (1.0 - soft_floor))
    inside = jnp.logical_and(sub < 7, lane < 127)
    previous = jnp.zeros((8, 128), jnp.float32)
    for z in range(8):
        if z < 7:
            picked = jnp.take_along_axis(table, cells_v[z], axis=1, mode="promise_in_bounds")
            s = jnp.where(inside, picked, 0.0)
        else:
            s = jnp.zeros((8, 128), jnp.float32)
        S[z, 4] = s
        s = s + roll(s, 1, 1)
        s = s + roll(s, 1, 0)
        S[z, 3] = s + previous
        previous = s
    loads[2].wait()
    for z in range(8):
        for c in range(3):
            S[z, c] = load_v[c, z]
    for f in range(4):
        YH[f] = jnp.concatenate([S[z, f, 7:8, :] for z in range(8)], axis=0)
        YLO[f] = jnp.concatenate([S[z, f, 0:1, :] for z in range(8)], axis=0)
        YLO[4 + f] = jnp.concatenate([S[z, f, 1:2, :] for z in range(8)], axis=0)
    YLO[8] = jnp.concatenate([S[z, 4, 0:1, :] for z in range(8)], axis=0)

    pl.semaphore_wait(barrier, awaited)

    def remote(source, target, sends, recvs, index, device):
        return pltpu.make_async_remote_copy(
            src_ref=source, dst_ref=target, send_sem=sends.at[index], recv_sem=recvs.at[index],
            device_id=device, device_id_type=MESH,
        )

    source_of = {
        (0, -1): S.at[pl.ds(0, 2)],
        (0, 1): S.at[7, pl.ds(0, 4)],
        (-1, 0): YLO,
        (1, 0): YH,
        (-1, -1): YLO.at[:, pl.ds(0, 2)],
        (-1, 1): YLO.at[pl.ds(0, 8), pl.ds(7, 1)],
        (1, -1): YH.at[:, pl.ds(0, 2)],
        (1, 1): YH.at[:, pl.ds(7, 1)],
    }
    y_copies = {
        (dy, dz): remote(source_of[dy, dz], side_buffer[-dy, -dz], y_send, y_recv, sides.index((dy, dz)), block_device(0, dy, dz))
        for dy, dz in sides
    }
    for dy, dz in sorted(sides, key=lambda side: -abs(side[0]) - abs(side[1])):
        @pl.when(both(dy, dz))
        def _(copy=y_copies[dy, dz]):
            copy.start()
    relay_tell(0)
    relay_wait(0)
    relay_tell(1)
    for dy, dz in sides:
        @pl.when(both(dy, dz))
        def _(copy=y_copies[-dy, -dz]):
            copy.wait_recv()

    top, bottom = sub == 0, sub == 7
    for f in range(4):
        low = YL[f] + jnp.where(top, wide(CLL[f]), 0.0) + jnp.where(bottom, wide(CLU[f, 0:1]), 0.0)
        low8 = CLU[f, 1:2]
        high = YU[f] + jnp.where(top, wide(CUL[f]), 0.0) + jnp.where(bottom, wide(CUU[f, 0:1]), 0.0)
        high8 = CUU[f, 1:2]
        G[f, 0:8] = YU[4 + f] + jnp.where(top, wide(CUL[4 + f]), 0.0) + jnp.where(bottom, wide(CUU[4 + f, 0:1]), 0.0)
        G[f, 8:9] = CUU[4 + f, 1:2]
        for z in range(9):
            tile = S[z, f] if z < 8 else ZU[1, f]
            if z == 0:
                tile = tile + ZL[f]
            if z == 7:
                tile = tile + ZU[0, f]
            lower = low[z : z + 1] if z < 8 else low8
            upper = high[z : z + 1] if z < 8 else high8
            A[z, f] = tile + jnp.where(top, wide(lower), 0.0) + jnp.where(bottom, wide(upper), 0.0)
    edge = YU[8]
    for z in range(8):
        tile = S[z, 4] if z < 7 else ZU[0, 4]
        row = edge[z : z + 1] if z < 7 else CUU[8, 0:1]
        A[z, 4] = jnp.where(bottom, wide(row), tile)

    low_tile = high_tile = jnp.zeros((8, 128), jnp.float32)
    low_row = high_row = jnp.zeros((1, 128), jnp.float32)
    for f in range(4):
        for z in range(9):
            k = 9 * f + z
            tile = roll(A[z, f], 3 * k - 125, 1)
            high_tile = jnp.where(third == k, tile, high_tile)
            low_tile = jnp.where(third == k + 1, tile, low_tile)
            row = roll(G[f, z : z + 1], 3 * k - 125, 1)
            high_row = jnp.where(third1 == k, row, high_row)
            low_row = jnp.where(third1 == k + 1, row, low_row)
    for z in range(8):
        tile = roll(A[z, 4], 108 + 2 * z - 125, 1)
        high_tile = jnp.where(lax.div(lane - 108, 2) == z if z else jnp.logical_or(lane == 108, lane == 109), tile, high_tile)
        low_tile = jnp.where(lax.div(lane - 111, 2) == z if z else jnp.logical_or(lane == 111, lane == 112), tile, low_tile)
    for buffer, tile, row in ((SL, high_tile, high_row), (SU, low_tile, low_row)):
        buffer[0:8] = tile
        buffer[8:9] = row
        buffer[9:16] = jnp.zeros((7, 128), jnp.float32)

    nine = pl.ds(0, 9)
    to_left = remote(SU.at[nine], SR.at[nine], x_send, x_recv, 0, block_device(-1, 0, 0))
    to_right = remote(SL.at[nine], SR.at[nine], x_send, x_recv, 1, block_device(1, 0, 0))

    @pl.when(gives_left)
    def _():
        to_left.start()

    @pl.when(gives_right)
    def _():
        relay_wait(1)
        to_right.start()

    keep = jnp.logical_or(lane > 0, gx > 0)
    keep1 = jnp.logical_or(lane1 > 0, gx > 0)
    inv_side = inverse(G[3, 0:8])
    inv_corner = inverse(G[3, 8:9])

    def along_x(p):
        q = roll(p, -1, 1)
        return p + q, q - p

    side = [along_x(jnp.where(keep, G[c, 0:8], 0.0) * inv_side) for c in range(3)]
    corner = [along_x(jnp.where(keep1, G[c, 8:9], 0.0) * inv_corner) for c in range(3)]
    owned = jnp.logical_and(
        jnp.logical_and(jnp.logical_or(lane > 1, gx == 0), jnp.logical_or(lane < 126, gx == NGX - 1)),
        jnp.logical_or(sub > 0, gy == 0),
    )
    owned_first = jnp.logical_and(owned, gz == 0)
    rz = jnp.zeros((8, 128), jnp.float32)
    for z in range(9):
        inv = inverse(A[z, 3])
        INV[z] = inv
        for c in range(3):
            start = jnp.where(keep, A[z, c], 0.0)
            p = start * inv
            if z < 8:
                A[z, c] = start
                rz = rz + jnp.where(owned if z else owned_first, start * p, 0.0)
            sums = along_x(p)
            for m in range(2):
                XM[z, c, m, 0:8] = sums[m]
                XM[z, c, m, 8:9] = side[c][m][z : z + 1] if z < 8 else corner[c][m]

    def plane_modes(z):
        modes = {}
        for c in range(3):
            for mx in range(2):
                here, above = XM[z, c, mx, 0:8], XM[z, c, mx, 1:9]
                modes[c, mx, 0] = here + above
                modes[c, mx, 1] = above - here
        return modes

    def spread(first, second, axis, mask):
        return first - second + jnp.where(mask, roll(first + second, 1, axis), 0.0)

    curvature = jnp.zeros((8, 128), jnp.float32)
    square = jnp.zeros((8, 128), jnp.float32)
    lower = plane_modes(0)
    carried = None
    for z in range(8):
        upper = plane_modes(z + 1)
        u = {}
        for key in lower:
            u[key + (0,)] = lower[key] + upper[key]
            u[key + (1,)] = upper[key] - lower[key]
        f = apply_modes(u, A[z, 4])
        here, carry = {}, {}
        for c in range(3):
            for mx in range(2):
                for my in range(2):
                    first, second = f[c, mx, my, 0], f[c, mx, my, 1]
                    if first is None:
                        here[c, mx, my], carry[c, mx, my] = -second, second
                    else:
                        here[c, mx, my], carry[c, mx, my] = first - second, first + second
        if carried is not None:
            here = {key: here[key] + carried[key] for key in here}
        carried = carry
        lower = upper
        inv = INV[z]
        mask = owned if z else owned_first
        for c in range(3):
            rows = [spread(here[c, mx, 0], here[c, mx, 1], 0, sub > 0) for mx in range(2)]
            image = jnp.where(keep, spread(rows[0], rows[1], 1, lane > 0), 0.0)
            IM[z, c] = image
            scaled = image * inv
            curvature = curvature + jnp.where(mask, A[z, c] * scaled, 0.0)
            square = square + jnp.where(mask, image * scaled, 0.0)

    @pl.when(jnp.logical_not(gives_right))
    def _():
        relay_wait(1)

    relay_tell(2)
    relay_wait(2)
    relay_tell(3)

    @pl.when(jnp.logical_and(has_face, jnp.logical_not(mirrored)))
    def _():
        to_left.wait_recv()

    @pl.when(jnp.logical_and(has_face, mirrored))
    def _():
        to_right.wait_recv()

    lane16 = lax.broadcasted_iota(jnp.int32, (16, 128), 1)
    sub16 = lax.broadcasted_iota(jnp.int32, (16, 128), 0)
    place = lax.rem(lane16, 64)
    column, layer = lax.rem(place, 3), lax.div(place, 3)
    counted = jnp.logical_and(
        jnp.logical_and(
            jnp.logical_and(sub16 < 8, jnp.logical_or(sub16 > 0, gy == 0)),
            jnp.logical_and(layer < 8, jnp.logical_or(layer > 0, gz == 0)),
        ),
        jnp.logical_and(has_face, jnp.where(lane16 < 64, column, 2 - 2 * jnp.abs(column - 1)) > 0),
    )
    received = SR[...]
    sums, for_lower, for_upper = strip_sums(
        jnp.where(mirrored, received, SL[...]), jnp.where(mirrored, SU[...], received), counted
    )
    rz, curvature, square = (
        total_of(own + part[0:8] + part[8:16]) for own, part in zip((rz, curvature, square), sums)
    )

    row = jnp.where(lane1 == 0, rz, jnp.where(lane1 == 1, curvature, square))
    rows_v[0:1] = row
    RA[0:1] = row
    def hops(k):
        return min(k % 4, 4 - k % 4) + min(k // 4, 4 - k // 4)

    for k in sorted(range(NGY), key=lambda k: -hops(k)):
        for flip in (True, False):
            if k or flip:
                device = plane_device(k // 4, k % 4, flip) if NGY == 16 else row_device(k, flip)
                slot = k + (NGY if flip else 0)
                remote(rows_v.at[pl.ds(0, 1)], RA.at[pl.ds(slot, 1)], a_send, a_recv, 0, device).start()

    RS[0] = for_lower
    RS[1] = for_upper
    result_right = remote(RS.at[1], LOW, f_send, f_recv, 3, block_device(1, 0, 0))
    result_left = remote(RS.at[0], HIGH, f_send, f_recv, 4, block_device(-1, 0, 0))
    normal_face = jnp.logical_and(has_face, jnp.logical_not(mirrored))
    mirrored_face = jnp.logical_and(has_face, mirrored)

    @pl.when(normal_face)
    def _():
        result_right.start()
        HIGH[...] = for_lower

    @pl.when(mirrored_face)
    def _():
        result_left.start()
        LOW[...] = for_upper

    def drain(ref, count, semaphore):
        block = ref.at[pl.ds(0, count)]
        pltpu.make_async_copy(block, block, semaphore).wait()

    drain(RA, 2 * NGY - 1, a_recv.at[0])
    row = jnp.sum(RA[...], axis=0, keepdims=True)
    rows_v[1:2] = row
    RB[along] = row
    relay_wait(3)
    for k in range(ring - 1):
        chip = jnp.where(k < along, k, k + 1)
        device = {"gx": div(chip, NGZ) * 2 + core, "gy": gy, "gz": rem(chip, NGZ)}
        remote(rows_v.at[pl.ds(1, 1)], RB.at[along], a_send, a_recv, 1, device).start()

    @pl.when(gives_left)
    def _():
        result_right.wait_recv()

    @pl.when(jnp.logical_or(gives_left, mirrored_face))
    def _():
        tile = LOW[...]
        for z in range(8):
            diagonal = roll(tile, -(72 + 3 * z), 1)
            INV[z] = jnp.where(lane == 0, inverse(diagonal), INV[z])
            for c in range(3):
                k = 24 * c + 3 * z
                IM[z, c] = jnp.where(lane < 2, roll(tile, -k, 1), IM[z, c])
                A[z, c] = jnp.where(lane == 0, roll(tile, -(k + 2), 1), A[z, c])

    @pl.when(gives_right)
    def _():
        result_left.wait_recv()

    @pl.when(jnp.logical_or(gives_right, normal_face))
    def _():
        tile = HIGH[...]
        for z in range(8):
            diagonal = roll(tile, 127 - (72 + 3 * z + 2), 1)
            INV[z] = jnp.where(lane == 127, inverse(diagonal), INV[z])
            for c in range(3):
                k = 24 * c + 3 * z
                IM[z, c] = jnp.where(lane > 125, roll(tile, 127 - (k + 2), 1), IM[z, c])
                A[z, c] = jnp.where(lane == 127, roll(tile, 127 - k, 1), A[z, c])

    for c in range(3):
        FYS[c] = jnp.concatenate([IM[z, c, 7:8, :] for z in range(8)], axis=0)
    z_fix = remote(IM.at[7], FZ, f_send, f_recv, 0, block_device(0, 0, 1))
    y_fix = remote(FYS, FY, f_send, f_recv, 1, block_device(0, 1, 0))
    yz_fix = remote(FYS.at[:, pl.ds(7, 1)], FYZ, f_send, f_recv, 2, block_device(0, 1, 1))
    fixes = ((yz_fix, 1, 1), (y_fix, 1, 0), (z_fix, 0, 1))
    for copy, dy, dz in fixes:
        @pl.when(both(dy, dz))
        def _(copy=copy):
            copy.start()
    for dy, dz in sides:
        @pl.when(both(dy, dz))
        def _(copy=y_copies[dy, dz]):
            copy.wait_send()
    for copy, dy, dz in fixes:
        @pl.when(both(-dy, -dz))
        def _(copy=copy):
            copy.wait_recv()
    for copy, dy, dz in fixes:
        @pl.when(both(dy, dz))
        def _(copy=copy):
            copy.wait_send()

    @pl.when(gz > 0)
    def _():
        IM[0] = FZ[...]

    @pl.when(gy > 0)
    def _():
        for c in range(3):
            for z in range(8):
                IM[z, c, 0:1, :] = FY[c, z : z + 1, :]

    @pl.when(both(-1, -1))
    def _():
        for c in range(3):
            IM[0, c, 0:1, :] = FYZ[c]

    for copy, condition in (
        (to_left, gives_left), (to_right, gives_right), (result_right, normal_face), (result_left, mirrored_face),
    ):
        @pl.when(condition)
        def _(copy=copy):
            copy.wait_send()
    drain(RA, 2 * NGY - 1, a_send.at[0])
    drain(RB, ring - 1, a_recv.at[1])
    row = jnp.sum(RB[...], axis=0)
    rz, curvature, square = (row[:, i : i + 1] for i in range(3))
    alpha = rz / curvature
    beta = alpha * alpha * square / rz - 1.0
    alpha, beta = wide(alpha), wide(beta)
    for z in range(8):
        inv = INV[z]
        for c in range(3):
            start = A[z, c]
            p = start * inv
            residual = start - alpha * IM[z, c]
            displacement_ref[c, z] = alpha * p
            residual_ref[c, z] = residual
            direction_ref[c, z] = residual * inv + beta * p
    drain(RB, ring - 1, a_send.at[1])


def store_kernel(a_ref, b_ref, c_ref, a_out, b_out, c_out, sem):
    copies = [
        pltpu.make_async_copy(source, target, sem.at[i])
        for i, (source, target) in enumerate(((a_ref, a_out), (b_ref, b_out), (c_ref, c_out)))
    ]
    for copy in copies:
        copy.start()
    for copy in copies:
        copy.wait()


def on_device(shape, load, classes, densities):
    f32, i32 = jnp.float32, jnp.int32
    ring = shape[0] // 2 * shape[2]
    dma = pltpu.SemaphoreType.DMA

    def rows(n):
        return pltpu.VMEM((n, 128), f32)

    def tiles(*dims):
        return pltpu.VMEM(dims + (8, 128), f32)

    out = jax.ShapeDtypeStruct(load.shape, f32)
    outs = pl.pallas_call(
        functools.partial(kernel, shape),
        out_shape=(out, out, out),
        in_specs=[pl.BlockSpec(memory_space=pltpu.HBM)] * 3,
        out_specs=(pl.BlockSpec(memory_space=pltpu.VMEM),) * 3,
        scratch_shapes=[
            pltpu.VMEM(load.shape, f32), pltpu.VMEM(classes.shape, i32), pltpu.VMEM((1, 64), f32), pltpu.VMEM((7, 8, 128), i32),
            tiles(8, 5), tiles(4), tiles(2, 5), tiles(4), tiles(9), tiles(4), tiles(9),
            pltpu.VMEM((4, 1, 128), f32), pltpu.VMEM((4, 2, 128), f32), pltpu.VMEM((8, 1, 128), f32), pltpu.VMEM((9, 2, 128), f32),
            tiles(9, 5), pltpu.VMEM((4, 16, 128), f32), rows(16), rows(16), rows(16),
            pltpu.VMEM((9, 3, 2, 16, 128), f32), tiles(8, 3), tiles(9),
            tiles(3), tiles(3), tiles(3), pltpu.VMEM((3, 1, 128), f32), tiles(2), tiles(), tiles(),
            rows(2 * shape[1]), pltpu.VMEM((ring, 1, 128), f32), rows(2),
            dma((3,)), dma((8,)), dma((8,)), dma((2,)), dma((2,)), dma((5,)), dma((5,)), dma((2,)), dma((2,)),
            pltpu.SemaphoreType.REGULAR((4,)),
        ],
        compiler_params=pltpu.CompilerParams(collective_id=0, has_side_effects=True, vmem_limit_bytes=8 * 2**20),
        name="step",
    )(*(pltpu.with_memory_space_constraint(x, pltpu.HBM) for x in (load, classes, densities.reshape(1, 64))))
    return pl.pallas_call(
        store_kernel,
        out_shape=(out, out, out),
        in_specs=[pl.BlockSpec(memory_space=pltpu.VMEM)] * 3,
        out_specs=(pl.BlockSpec(memory_space=pl.ANY),) * 3,
        scratch_shapes=[dma((3,))],
        compiler_params=pltpu.CompilerParams(vmem_limit_bytes=2 * 2**20),
        name="store",
    )(*outs)


def solution(mesh):
    shape = tuple(mesh.shape[a] for a in ("gx", "gy", "gz"))
    spec = P(None, "gz", "gy", "gx")
    return jax.shard_map(
        functools.partial(on_device, shape), mesh=mesh,
        in_specs=(spec, P("gz", "gy", "gx"), P()), out_specs=(spec, spec, spec), check_vma=False,
    )
```

```python
import functools
import math

import jax
import jax.numpy as jnp
import numpy as np
from jax import lax
from jax.experimental import pallas as pl
from jax.experimental.pallas import tpu as pltpu
from jax.sharding import PartitionSpec as P

MESH = pl.DeviceIdType.MESH
soft_floor = 0.001
poisson = 0.3
lame = poisson / ((1.0 + poisson) * (1.0 - 2.0 * poisson))
shear = 0.5 / (1.0 + poisson)

MASS = (0.25, 1.0 / 12.0)
MODES = [(mx, my, mz) for mx in (0, 1) for my in (0, 1) for mz in (0, 1)]


def mode_couplings():
    rows = {(c, m): [] for c in range(3) for m in MODES}
    for c in range(3):
        for m in MODES:
            own = 0.0
            for axis in range(3):
                if m[axis] == 1:
                    factor = lame + 2.0 * shear if axis == c else shear
                    others = [MASS[m[o]] for o in range(3) if o != axis]
                    own += factor * others[0] * others[1]
            if own:
                rows[c, m].append((own, c, m))
            for k in range(3):
                if k == c:
                    continue
                rest = 3 - c - k
                if m[c] == 1 and m[k] == 0:
                    factor = lame
                elif m[c] == 0 and m[k] == 1:
                    factor = shear
                else:
                    continue
                partner = list(m)
                partner[c], partner[k] = m[k], m[c]
                rows[c, m].append((factor * 0.25 * MASS[m[rest]], k, tuple(partner)))
    return rows


COUPLINGS = mode_couplings()
CORNER_DIAGONAL = sum(w for m in MODES for w, c, _ in COUPLINGS[0, m] if c == 0)


def apply_modes(u, s):
    out = {}
    for c in range(3):
        for m in MODES:
            total = None
            for weight, k, partner in COUPLINGS[c, m]:
                term = u[(k,) + partner] * weight
                total = term if total is None else total + term
            out[(c,) + m] = None if total is None else total * s
    return out


def roll(v, shift, axis):
    return pltpu.roll(v, shift % v.shape[axis], axis)


def inverse(d):
    return 1.0 / jnp.where(d > 0.0, d * CORNER_DIAGONAL, 1.0)


def wide(tile):
    return jnp.broadcast_to(tile, (8, 128))


def total_of(tile):
    return jnp.sum(jnp.sum(tile, axis=0, keepdims=True), axis=1, keepdims=True)


def div(a, n):
    return a >> (n.bit_length() - 1) if n & (n - 1) == 0 else lax.div(a, n)


def rem(a, n):
    return a & (n - 1) if n & (n - 1) == 0 else lax.rem(a, n)


def strip_sums(lower, upper, counted):
    lane = lax.broadcasted_iota(jnp.int32, (16, 128), 1)
    first = lane < 64
    place = lax.rem(lane, 64)
    column, layer = lax.rem(place, 3), lax.div(place, 3)

    def shared(v):
        joined = v + jnp.where(first, roll(v, -62, 1), roll(v, 62, 1))
        return jnp.where(column == jnp.where(first, 2, 0), joined, v)

    def field(f):
        return jnp.where(first, roll(lower, -27 * f, 1), roll(upper, 61 - 27 * f, 1))

    s = jnp.zeros((8, 128), jnp.float32)
    for z in range(8):
        found = jnp.where(first[0:8], roll(lower[0:8], z - 108, 1), roll(upper[0:8], z - 111 + 64, 1))
        s = jnp.where(jnp.logical_and(layer[0:8] == z, column[0:8] < 2), found, s)
    s = jnp.concatenate([s, jnp.zeros((8, 128), jnp.float32)], axis=0)
    d = shared(field(3))
    inv = inverse(d)
    starts, vectors, u = [], [], {}
    for c in range(3):
        start = shared(field(c))
        p = start * inv
        starts.append(start)
        vectors.append(p)
        q = roll(p, -1, 1)
        for mx, along_x in enumerate((p + q, q - p)):
            q = roll(along_x, -1, 0)
            for my, along_y in enumerate((along_x + q, q - along_x)):
                q = roll(along_y, -3, 1)
                u[c, mx, my, 0] = along_y + q
                u[c, mx, my, 1] = q - along_y
    f = apply_modes(u, s)
    rz = curvature = square = jnp.zeros((16, 128), jnp.float32)
    parts = []

    def back(a, b, shift, axis):
        low, high = (-b, b) if a is None else (a - b, a + b)
        return low + roll(high, shift, axis)

    for c in range(3):
        x_parts = []
        for mx in range(2):
            y_parts = [back(f[c, mx, my, 0], f[c, mx, my, 1], 3, 1) for my in range(2)]
            x_parts.append(back(y_parts[0], y_parts[1], 1, 0))
        image = shared(back(x_parts[0], x_parts[1], 1, 1))
        scaled = image * inv
        rz = rz + jnp.where(counted, starts[c] * vectors[c], 0.0)
        curvature = curvature + jnp.where(counted, vectors[c] * image, 0.0)
        square = square + jnp.where(counted, image * scaled, 0.0)
        parts.append((image[0:8], starts[c][0:8]))
    return (rz, curvature, square), (parts, d[0:8])


def strip_results(parts, d):
    lane = lax.broadcasted_iota(jnp.int32, (8, 128), 1)
    first = lane < 64
    column = lax.rem(lax.rem(lane, 64), 3)
    tiles = []
    for image, start in parts:
        moved = jnp.where(first, roll(start, -2, 1), roll(start, 2, 1))
        tiles.append(jnp.where(column == jnp.where(first, 0, 2), moved, image))
    tiles.append(d)
    for_lower = for_upper = jnp.zeros((8, 128), jnp.float32)
    for i, tile in enumerate(tiles):
        here = lax.div(lane, 24) == i
        for_lower = jnp.where(here, roll(tile, 24 * i, 1), for_lower)
        for_upper = jnp.where(here, roll(tile, 24 * i - 64, 1), for_upper)
    return for_lower, for_upper


def kernel(
    shape,
    load_hbm, classes_hbm, densities_hbm,
    displacement_ref, residual_ref, direction_ref,
    load_v, classes_v, table_v, cells_v,
    S, ZL, ZU, YH, YLO, YL, YU, CLL, CLU, CUL, CUU,
    A, G, SL, SU, SR, XM, IM, INV, FZ, FYS, FY, FYZ, RS, LOW, HIGH,
    RA, RB, rows_v,
    in_sem, y_send, y_recv, x_send, x_recv, f_send, f_recv, a_send, a_recv, relay,
):
    NGX, NGY, NGZ = shape
    ring = NGX // 2 * NGZ
    gx, gy, gz = (lax.axis_index(a) for a in ("gx", "gy", "gz"))
    core = rem(gx, 2)
    along = div(gx, 2) * NGZ + gz
    pivot = jnp.where(gz < 5 * NGZ // 8, NGX - 2, NGX - 4)
    mirrored = gx >= pivot
    has_face = jnp.logical_or(jnp.logical_and(mirrored, gx > 0), gx < pivot - 1)
    gives_left = jnp.logical_and(gx >= 1, gx <= pivot - 1)
    gives_right = jnp.logical_and(gx >= pivot - 1, gx <= NGX - 2)

    def both(dy, dz):
        terms = []
        if dy:
            terms.append(gy > 0 if dy < 0 else gy < NGY - 1)
        if dz:
            terms.append(gz > 0 if dz < 0 else gz < NGZ - 1)
        return terms[0] if len(terms) == 1 else jnp.logical_and(terms[0], terms[1])

    def ring_device(offset, flip=False):
        q = rem(along + (offset % ring), ring)
        c = 1 - core if flip else core
        return {"gx": div(q, NGZ) * 2 + c, "gy": gy, "gz": rem(q, NGZ)}

    def row_device(offset, flip=False):
        c = 1 - core if flip else core
        return {"gx": gx - core + c, "gy": rem(gy + offset, NGY), "gz": gz}

    def plane_device(dy, dx, flip=False):
        y, x = rem(div(gy, 4) + dy, 4), rem(rem(gy, 4) + dx, 4)
        c = 1 - core if flip else core
        return {"gx": gx - core + c, "gy": y * 4 + x, "gz": gz}

    def block_device(dx, dy, dz):
        return {"gx": gx + dx, "gy": gy + dy, "gz": gz + dz}

    sides = [(dy, dz) for dy in (-1, 0, 1) for dz in (-1, 0, 1) if (dy, dz) != (0, 0)]
    side_buffer = {
        (0, -1): ZL, (0, 1): ZU, (-1, 0): YL, (1, 0): YU,
        (-1, -1): CLL, (-1, 1): CLU, (1, -1): CUL, (1, 1): CUU,
    }

    loads = [
        pltpu.make_async_copy(classes_hbm, classes_v, in_sem.at[0]),
        pltpu.make_async_copy(densities_hbm, table_v, in_sem.at[1]),
        pltpu.make_async_copy(load_hbm, load_v, in_sem.at[2]),
    ]
    for copy in loads:
        copy.start()

    for (dy, dz), buffer in side_buffer.items():
        @pl.when(jnp.logical_not(both(dy, dz)))
        def _(buffer=buffer):
            buffer[...] = jnp.zeros_like(buffer)
    SR[...] = jnp.zeros_like(SR)

    barrier = pltpu.get_barrier_semaphore()

    def tell(device, semaphore):
        pl.semaphore_signal(semaphore, inc=1, device_id=device, device_id_type=MESH)

    two_away = [ring_device(o, flip) for o in sorted({2, ring - 2}) for flip in (False, True)]
    one_away = [ring_device(o) for o in (1, -1)] if ring > 2 else []
    if NGY == 16:
        plane = [plane_device(*o) for o in ((0, 1), (0, 3), (1, 0), (3, 0))]
        plane_far = [plane_device(*o) for o in ((0, 2), (2, 0))]
    else:
        plane, plane_far = [row_device(o) for o in range(1, NGY)], []
    flipped = row_device(0, True)
    relays = [
        ([ring_device(o, flip) for o in (2, -2) for flip in (False, True)] if ring >= 8 else []) + plane,
        ([ring_device(o, flip) for o in (4, -4) for flip in (False, True)] if ring >= 16 else []) + plane_far,
        [flipped],
        [ring_device(o) for o in (8, -8)] if ring >= 32 else [],
    ]

    def relay_tell(step):
        for device in relays[step]:
            tell(device, relay.at[step])

    def relay_wait(step):
        if relays[step]:
            pl.semaphore_wait(relay.at[step], len(relays[step]))

    @pl.when(jnp.logical_and(gx < pivot - 1, core == 1))
    def _():
        tell(block_device(1, 0, 0), barrier)

    awaited = jnp.logical_and(gives_left, core == 0).astype(jnp.int32)

    def tell_side(dy, dz):
        @pl.when(both(dy, dz))
        def _():
            tell(block_device(0, dy, dz), barrier)
        return both(dy, dz).astype(jnp.int32)

    for dy, dz in sides:
        if dy and dz:
            awaited = awaited + tell_side(dy, dz)
    for device in two_away:
        tell(device, barrier)
    for dy, dz in sides:
        if not (dy and dz):
            awaited = awaited + tell_side(dy, dz)
    for device in plane + one_away + [flipped]:
        tell(device, barrier)
    awaited = awaited + len(two_away + plane + one_away + [flipped])

    lane = lax.broadcasted_iota(jnp.int32, (8, 128), 1)
    sub = lax.broadcasted_iota(jnp.int32, (8, 128), 0)
    lane1 = lax.broadcasted_iota(jnp.int32, (1, 128), 1)
    third, third1 = lax.div(lane, 3), lax.div(lane1, 3)

    cells_v[...] = jnp.zeros_like(cells_v)
    loads[0].wait()
    cells_v[:, 0:7, 0:127] = classes_v[...]
    loads[1].wait()
    rho = table_v[...]
    rho = jnp.concatenate([rho, rho], axis=1)
    table = wide(soft_floor + rho * rho * rho * (1.0 - soft_floor))
    inside = jnp.logical_and(sub < 7, lane < 127)
    previous = jnp.zeros((8, 128), jnp.float32)
    for z in range(8):
        if z < 7:
            picked = jnp.take_along_axis(table, cells_v[z], axis=1, mode="promise_in_bounds")
            s = jnp.where(inside, picked, 0.0)
        else:
            s = jnp.zeros((8, 128), jnp.float32)
        S[z, 4] = s
        s = s + roll(s, 1, 1)
        s = s + roll(s, 1, 0)
        S[z, 3] = s + previous
        previous = s
    loads[2].wait()
    for z in range(8):
        for c in range(3):
            S[z, c] = load_v[c, z]
    for f in range(4):
        YH[f] = jnp.concatenate([S[z, f, 7:8, :] for z in range(8)], axis=0)
        YLO[f] = jnp.concatenate([S[z, f, 0:1, :] for z in range(8)], axis=0)
        YLO[4 + f] = jnp.concatenate([S[z, f, 1:2, :] for z in range(8)], axis=0)
    YLO[8] = jnp.concatenate([S[z, 4, 0:1, :] for z in range(8)], axis=0)

    pl.semaphore_wait(barrier, awaited)

    def remote(source, target, sends, recvs, index, device):
        return pltpu.make_async_remote_copy(
            src_ref=source, dst_ref=target, send_sem=sends.at[index], recv_sem=recvs.at[index],
            device_id=device, device_id_type=MESH,
        )

    source_of = {
        (0, -1): S.at[pl.ds(0, 2)],
        (0, 1): S.at[7, pl.ds(0, 4)],
        (-1, 0): YLO,
        (1, 0): YH,
        (-1, -1): YLO.at[:, pl.ds(0, 2)],
        (-1, 1): YLO.at[pl.ds(0, 8), pl.ds(7, 1)],
        (1, -1): YH.at[:, pl.ds(0, 2)],
        (1, 1): YH.at[:, pl.ds(7, 1)],
    }
    y_copies = {
        (dy, dz): remote(source_of[dy, dz], side_buffer[-dy, -dz], y_send, y_recv, sides.index((dy, dz)), block_device(0, dy, dz))
        for dy, dz in sides
    }
    for dy, dz in sorted(sides, key=lambda side: -abs(side[0]) - abs(side[1])):
        @pl.when(both(dy, dz))
        def _(copy=y_copies[dy, dz]):
            copy.start()
    relay_tell(0)
    relay_wait(0)
    relay_tell(1)
    for dy, dz in sides:
        @pl.when(both(dy, dz))
        def _(copy=y_copies[-dy, -dz]):
            copy.wait_recv()

    top, bottom = sub == 0, sub == 7
    for f in range(4):
        low = YL[f] + jnp.where(top, wide(CLL[f]), 0.0) + jnp.where(bottom, wide(CLU[f, 0:1]), 0.0)
        low8 = CLU[f, 1:2]
        high = YU[f] + jnp.where(top, wide(CUL[f]), 0.0) + jnp.where(bottom, wide(CUU[f, 0:1]), 0.0)
        high8 = CUU[f, 1:2]
        G[f, 0:8] = YU[4 + f] + jnp.where(top, wide(CUL[4 + f]), 0.0) + jnp.where(bottom, wide(CUU[4 + f, 0:1]), 0.0)
        G[f, 8:9] = CUU[4 + f, 1:2]
        for z in range(9):
            tile = S[z, f] if z < 8 else ZU[1, f]
            if z == 0:
                tile = tile + ZL[f]
            if z == 7:
                tile = tile + ZU[0, f]
            lower = low[z : z + 1] if z < 8 else low8
            upper = high[z : z + 1] if z < 8 else high8
            A[z, f] = tile + jnp.where(top, wide(lower), 0.0) + jnp.where(bottom, wide(upper), 0.0)
    edge = YU[8]
    for z in range(8):
        tile = S[z, 4] if z < 7 else ZU[0, 4]
        row = edge[z : z + 1] if z < 7 else CUU[8, 0:1]
        A[z, 4] = jnp.where(bottom, wide(row), tile)

    low_tile = high_tile = jnp.zeros((8, 128), jnp.float32)
    low_row = high_row = jnp.zeros((1, 128), jnp.float32)
    for f in range(4):
        for z in range(9):
            k = 9 * f + z
            tile = roll(A[z, f], 3 * k - 125, 1)
            high_tile = jnp.where(third == k, tile, high_tile)
            low_tile = jnp.where(third == k + 1, tile, low_tile)
            row = roll(G[f, z : z + 1], 3 * k - 125, 1)
            high_row = jnp.where(third1 == k, row, high_row)
            low_row = jnp.where(third1 == k + 1, row, low_row)
    for z in range(8):
        tile = roll(A[z, 4], 108 + 2 * z - 125, 1)
        high_tile = jnp.where(lax.div(lane - 108, 2) == z if z else jnp.logical_or(lane == 108, lane == 109), tile, high_tile)
        low_tile = jnp.where(lax.div(lane - 111, 2) == z if z else jnp.logical_or(lane == 111, lane == 112), tile, low_tile)
    for buffer, tile, row in ((SL, high_tile, high_row), (SU, low_tile, low_row)):
        buffer[0:8] = tile
        buffer[8:9] = row
        buffer[9:16] = jnp.zeros((7, 128), jnp.float32)

    nine = pl.ds(0, 9)
    to_left = remote(SU.at[nine], SR.at[nine], x_send, x_recv, 0, block_device(-1, 0, 0))
    to_right = remote(SL.at[nine], SR.at[nine], x_send, x_recv, 1, block_device(1, 0, 0))

    @pl.when(gives_left)
    def _():
        to_left.start()

    @pl.when(gives_right)
    def _():
        relay_wait(1)
        to_right.start()

    keep = jnp.logical_or(lane > 0, gx > 0)
    keep1 = jnp.logical_or(lane1 > 0, gx > 0)
    inv_side = inverse(G[3, 0:8])
    inv_corner = inverse(G[3, 8:9])

    def along_x(p):
        q = roll(p, -1, 1)
        return p + q, q - p

    side = [along_x(jnp.where(keep, G[c, 0:8], 0.0) * inv_side) for c in range(3)]
    corner = [along_x(jnp.where(keep1, G[c, 8:9], 0.0) * inv_corner) for c in range(3)]
    owned = jnp.logical_and(
        jnp.logical_and(jnp.logical_or(lane > 1, gx == 0), jnp.logical_or(lane < 126, gx == NGX - 1)),
        jnp.logical_or(sub > 0, gy == 0),
    )
    owned_first = jnp.logical_and(owned, gz == 0)
    rz = jnp.zeros((8, 128), jnp.float32)
    for z in range(9):
        inv = inverse(A[z, 3])
        INV[z] = inv
        for c in range(3):
            start = jnp.where(keep, A[z, c], 0.0)
            p = start * inv
            if z < 8:
                A[z, c] = start
                rz = rz + jnp.where(owned if z else owned_first, start * p, 0.0)
            sums = along_x(p)
            for m in range(2):
                XM[z, c, m, 0:8] = sums[m]
                XM[z, c, m, 8:9] = side[c][m][z : z + 1] if z < 8 else corner[c][m]

    def plane_modes(z):
        modes = {}
        for c in range(3):
            for mx in range(2):
                here, above = XM[z, c, mx, 0:8], XM[z, c, mx, 1:9]
                modes[c, mx, 0] = here + above
                modes[c, mx, 1] = above - here
        return modes

    def spread(first, second, axis, mask):
        return first - second + jnp.where(mask, roll(first + second, 1, axis), 0.0)

    curvature = jnp.zeros((8, 128), jnp.float32)
    square = jnp.zeros((8, 128), jnp.float32)
    lower = plane_modes(0)
    carried = None
    for z in range(8):
        upper = plane_modes(z + 1)
        u = {}
        for key in lower:
            u[key + (0,)] = lower[key] + upper[key]
            u[key + (1,)] = upper[key] - lower[key]
        f = apply_modes(u, A[z, 4])
        here, carry = {}, {}
        for c in range(3):
            for mx in range(2):
                for my in range(2):
                    first, second = f[c, mx, my, 0], f[c, mx, my, 1]
                    if first is None:
                        here[c, mx, my], carry[c, mx, my] = -second, second
                    else:
                        here[c, mx, my], carry[c, mx, my] = first - second, first + second
        if carried is not None:
            here = {key: here[key] + carried[key] for key in here}
        carried = carry
        lower = upper
        inv = INV[z]
        mask = owned if z else owned_first
        for c in range(3):
            rows = [spread(here[c, mx, 0], here[c, mx, 1], 0, sub > 0) for mx in range(2)]
            image = jnp.where(keep, spread(rows[0], rows[1], 1, lane > 0), 0.0)
            IM[z, c] = image
            scaled = image * inv
            curvature = curvature + jnp.where(mask, A[z, c] * scaled, 0.0)
            square = square + jnp.where(mask, image * scaled, 0.0)

    @pl.when(jnp.logical_not(gives_right))
    def _():
        relay_wait(1)

    relay_tell(2)
    relay_wait(2)
    relay_tell(3)

    @pl.when(jnp.logical_and(has_face, jnp.logical_not(mirrored)))
    def _():
        to_left.wait_recv()

    @pl.when(jnp.logical_and(has_face, mirrored))
    def _():
        to_right.wait_recv()

    lane16 = lax.broadcasted_iota(jnp.int32, (16, 128), 1)
    sub16 = lax.broadcasted_iota(jnp.int32, (16, 128), 0)
    place = lax.rem(lane16, 64)
    column, layer = lax.rem(place, 3), lax.div(place, 3)
    counted = jnp.logical_and(
        jnp.logical_and(
            jnp.logical_and(sub16 < 8, jnp.logical_or(sub16 > 0, gy == 0)),
            jnp.logical_and(layer < 8, jnp.logical_or(layer > 0, gz == 0)),
        ),
        jnp.logical_and(has_face, jnp.where(lane16 < 64, column, 2 - 2 * jnp.abs(column - 1)) > 0),
    )
    received = SR[...]
    sums, found = strip_sums(
        jnp.where(mirrored, received, SL[...]), jnp.where(mirrored, SU[...], received), counted
    )
    rz, curvature, square = (
        total_of(own + part[0:8] + part[8:16]) for own, part in zip((rz, curvature, square), sums)
    )

    row = jnp.where(lane1 == 0, rz, jnp.where(lane1 == 1, curvature, square))
    rows_v[0:1] = row
    RA[0:1] = row
    def hops(k):
        return min(k % 4, 4 - k % 4) + min(k // 4, 4 - k // 4)

    for k in sorted(range(NGY), key=lambda k: -hops(k)):
        for flip in (True, False):
            if k or flip:
                device = plane_device(k // 4, k % 4, flip) if NGY == 16 else row_device(k, flip)
                slot = k + (NGY if flip else 0)
                remote(rows_v.at[pl.ds(0, 1)], RA.at[pl.ds(slot, 1)], a_send, a_recv, 0, device).start()

    for_lower, for_upper = strip_results(*found)
    RS[0] = for_lower
    RS[1] = for_upper
    result_right = remote(RS.at[1], LOW, f_send, f_recv, 3, block_device(1, 0, 0))
    result_left = remote(RS.at[0], HIGH, f_send, f_recv, 4, block_device(-1, 0, 0))
    normal_face = jnp.logical_and(has_face, jnp.logical_not(mirrored))
    mirrored_face = jnp.logical_and(has_face, mirrored)

    @pl.when(normal_face)
    def _():
        result_right.start()
        HIGH[...] = for_lower

    @pl.when(mirrored_face)
    def _():
        result_left.start()
        LOW[...] = for_upper

    def drain(ref, count, semaphore):
        block = ref.at[pl.ds(0, count)]
        pltpu.make_async_copy(block, block, semaphore).wait()

    drain(RA, 2 * NGY - 1, a_recv.at[0])
    row = jnp.sum(RA[...], axis=0, keepdims=True)
    rows_v[1:2] = row
    RB[along] = row
    relay_wait(3)
    for k in range(ring - 1):
        chip = jnp.where(k < along, k, k + 1)
        device = {"gx": div(chip, NGZ) * 2 + core, "gy": gy, "gz": rem(chip, NGZ)}
        remote(rows_v.at[pl.ds(1, 1)], RB.at[along], a_send, a_recv, 1, device).start()

    @pl.when(gives_left)
    def _():
        result_right.wait_recv()

    @pl.when(jnp.logical_or(gives_left, mirrored_face))
    def _():
        tile = LOW[...]
        for z in range(8):
            diagonal = roll(tile, -(72 + 3 * z), 1)
            INV[z] = jnp.where(lane == 0, inverse(diagonal), INV[z])
            for c in range(3):
                k = 24 * c + 3 * z
                IM[z, c] = jnp.where(lane < 2, roll(tile, -k, 1), IM[z, c])
                A[z, c] = jnp.where(lane == 0, roll(tile, -(k + 2), 1), A[z, c])

    @pl.when(gives_right)
    def _():
        result_left.wait_recv()

    @pl.when(jnp.logical_or(gives_right, normal_face))
    def _():
        tile = HIGH[...]
        for z in range(8):
            diagonal = roll(tile, 127 - (72 + 3 * z + 2), 1)
            INV[z] = jnp.where(lane == 127, inverse(diagonal), INV[z])
            for c in range(3):
                k = 24 * c + 3 * z
                IM[z, c] = jnp.where(lane > 125, roll(tile, 127 - (k + 2), 1), IM[z, c])
                A[z, c] = jnp.where(lane == 127, roll(tile, 127 - k, 1), A[z, c])

    for c in range(3):
        FYS[c] = jnp.concatenate([IM[z, c, 7:8, :] for z in range(8)], axis=0)
    z_fix = remote(IM.at[7], FZ, f_send, f_recv, 0, block_device(0, 0, 1))
    y_fix = remote(FYS, FY, f_send, f_recv, 1, block_device(0, 1, 0))
    yz_fix = remote(FYS.at[:, pl.ds(7, 1)], FYZ, f_send, f_recv, 2, block_device(0, 1, 1))
    fixes = ((yz_fix, 1, 1), (y_fix, 1, 0), (z_fix, 0, 1))
    for copy, dy, dz in fixes:
        @pl.when(both(dy, dz))
        def _(copy=copy):
            copy.start()
    for dy, dz in sides:
        @pl.when(both(dy, dz))
        def _(copy=y_copies[dy, dz]):
            copy.wait_send()
    for copy, dy, dz in fixes:
        @pl.when(both(-dy, -dz))
        def _(copy=copy):
            copy.wait_recv()
    for copy, dy, dz in fixes:
        @pl.when(both(dy, dz))
        def _(copy=copy):
            copy.wait_send()

    @pl.when(gz > 0)
    def _():
        IM[0] = FZ[...]

    @pl.when(gy > 0)
    def _():
        for c in range(3):
            for z in range(8):
                IM[z, c, 0:1, :] = FY[c, z : z + 1, :]

    @pl.when(both(-1, -1))
    def _():
        for c in range(3):
            IM[0, c, 0:1, :] = FYZ[c]

    for copy, condition in (
        (to_left, gives_left), (to_right, gives_right), (result_right, normal_face), (result_left, mirrored_face),
    ):
        @pl.when(condition)
        def _(copy=copy):
            copy.wait_send()
    drain(RA, 2 * NGY - 1, a_send.at[0])
    drain(RB, ring - 1, a_recv.at[1])
    row = jnp.sum(RB[...], axis=0)
    rz, curvature, square = (row[:, i : i + 1] for i in range(3))
    alpha = rz / curvature
    beta = alpha * alpha * square / rz - 1.0
    alpha, beta = wide(alpha), wide(beta)
    for z in range(8):
        inv = INV[z]
        for c in range(3):
            start = A[z, c]
            p = start * inv
            residual = start - alpha * IM[z, c]
            displacement_ref[c, z] = alpha * p
            residual_ref[c, z] = residual
            direction_ref[c, z] = residual * inv + beta * p
    drain(RB, ring - 1, a_send.at[1])


def store_kernel(a_ref, b_ref, c_ref, a_out, b_out, c_out, sem):
    copies = [
        pltpu.make_async_copy(source, target, sem.at[i])
        for i, (source, target) in enumerate(((a_ref, a_out), (b_ref, b_out), (c_ref, c_out)))
    ]
    for copy in copies:
        copy.start()
    for copy in copies:
        copy.wait()


def on_device(shape, load, classes, densities):
    f32, i32 = jnp.float32, jnp.int32
    ring = shape[0] // 2 * shape[2]
    dma = pltpu.SemaphoreType.DMA

    def rows(n):
        return pltpu.VMEM((n, 128), f32)

    def tiles(*dims):
        return pltpu.VMEM(dims + (8, 128), f32)

    out = jax.ShapeDtypeStruct(load.shape, f32)
    outs = pl.pallas_call(
        functools.partial(kernel, shape),
        out_shape=(out, out, out),
        in_specs=[pl.BlockSpec(memory_space=pltpu.HBM)] * 3,
        out_specs=(pl.BlockSpec(memory_space=pltpu.VMEM),) * 3,
        scratch_shapes=[
            pltpu.VMEM(load.shape, f32), pltpu.VMEM(classes.shape, i32), pltpu.VMEM((1, 64), f32), pltpu.VMEM((7, 8, 128), i32),
            tiles(8, 5), tiles(4), tiles(2, 5), tiles(4), tiles(9), tiles(4), tiles(9),
            pltpu.VMEM((4, 1, 128), f32), pltpu.VMEM((4, 2, 128), f32), pltpu.VMEM((8, 1, 128), f32), pltpu.VMEM((9, 2, 128), f32),
            tiles(9, 5), pltpu.VMEM((4, 16, 128), f32), rows(16), rows(16), rows(16),
            pltpu.VMEM((9, 3, 2, 16, 128), f32), tiles(8, 3), tiles(9),
            tiles(3), tiles(3), tiles(3), pltpu.VMEM((3, 1, 128), f32), tiles(2), tiles(), tiles(),
            rows(2 * shape[1]), pltpu.VMEM((ring, 1, 128), f32), rows(2),
            dma((3,)), dma((8,)), dma((8,)), dma((2,)), dma((2,)), dma((5,)), dma((5,)), dma((2,)), dma((2,)),
            pltpu.SemaphoreType.REGULAR((4,)),
        ],
        compiler_params=pltpu.CompilerParams(collective_id=0, has_side_effects=True, vmem_limit_bytes=8 * 2**20),
        name="step",
    )(*(pltpu.with_memory_space_constraint(x, pltpu.HBM) for x in (load, classes, densities.reshape(1, 64))))
    return pl.pallas_call(
        store_kernel,
        out_shape=(out, out, out),
        in_specs=[pl.BlockSpec(memory_space=pltpu.VMEM)] * 3,
        out_specs=(pl.BlockSpec(memory_space=pl.ANY),) * 3,
        scratch_shapes=[dma((3,))],
        compiler_params=pltpu.CompilerParams(vmem_limit_bytes=2 * 2**20),
        name="store",
    )(*outs)


def solution(mesh):
    shape = tuple(mesh.shape[a] for a in ("gx", "gy", "gz"))
    spec = P(None, "gz", "gy", "gx")
    return jax.shard_map(
        functools.partial(on_device, shape), mesh=mesh,
        in_specs=(spec, P("gz", "gy", "gx"), P()), out_specs=(spec, spec, spec), check_vma=False,
    )
```
